512 devices in a mesh: wide: 64 (over z, y), narrow: 8 (over x, core).
Axes of the slice: x: 4, y: 8, z: 8, core: 2. Of those that a mesh axis runs over, the one named last changes fastest.
Arguments:
- velocity: bfloat16 [3, 512, 1024], P(None, 'wide', 'narrow'), may hold values from -6 to 6
- cotangent: bfloat16 [3, 512, 1024], P(None, 'wide', 'narrow'), may hold values from -6 to 6
- kernel_one: bfloat16 [27, 16, 3], replicated, may hold values from -0.625 to 0.625
- kernel_two: bfloat16 [27, 32, 16], replicated, may hold values from -0.3125 to 0.3125
- kernel_three: bfloat16 [27, 64, 32], replicated, may hold values from -0.21875 to 0.21875
- kernel_four: bfloat16 [27, 128, 64], replicated, may hold values from -0.15625 to 0.15625
- lift_four: bfloat16 [64, 128], replicated, may hold values from -0.5 to 0.5
- lift_three: bfloat16 [32, 64], replicated, may hold values from -0.75 to 0.75
- lift_two: bfloat16 [16, 32], replicated, may hold values from -1 to 1
- head: bfloat16 [3, 16], replicated, may hold values from -1.5 to 1.5
Outputs:
- prediction: float32 [3, 512, 1024], P(None, 'wide', 'narrow')
- grad_velocity: float32 [3, 512, 1024], P(None, 'wide', 'narrow')
- grad_kernel_one: float32 [27, 16, 3], replicated
- grad_kernel_two: float32 [27, 32, 16], replicated
- grad_kernel_three: float32 [27, 64, 32], replicated
- grad_kernel_four: float32 [27, 128, 64], replicated
- grad_lift_four: float32 [64, 128], replicated
- grad_lift_three: float32 [32, 64], replicated
- grad_lift_two: float32 [16, 32], replicated
- grad_head: float32 [3, 16], replicated
The draws below stay inside these ranges and needn't reach their ends.
All inputs are finite; a program needn't handle non-finite values.
Results may differ from the reference program's by a relative error of at most 0.012.
The reference program's roundings to bfloat16 on the way (of `shrink`) count: a program that leaves them out, or rounds other values in their place, can miss the bound.
Values may be sent and summed in bfloat16 or wider, within the bound.
No kernel may reach another device: no remote copies, remote signals or barrier semaphores. Data moves between devices by JAX's collectives and lax.ppermute only.
A program may use at most 64 MiB of HBM per device.

```python
import jax
import jax.numpy as jnp
from jax import lax

CIN = 3
TAPS = 27
C1 = 16
C2 = 32
C3 = 64
C4 = 128
NZ = 16
NX = 512
NY = 64


def steps_of(rng, shape, split, smallest, high):
    gain = 1.0
    for dim, shards_of in split:
        steps = jax.random.uniform(jax.random.fold_in(jax.random.fold_in(rng, 6), dim), (shards_of,), jnp.float32, smallest / len(split), high / len(split))
        gain = gain * jnp.repeat(jnp.exp(steps), shape[dim] // shards_of).reshape((-1,) + (1,) * (len(shape) - 1 - dim))
    return gain


def normal_values(key, shape, width, bound, cuts=(), kind=jnp.bfloat16):
    level = steps_of(key, shape, cuts, -0.22, 0.18) if cuts else 1.0
    result = jax.random.normal(key, shape, jnp.float32) * width * level
    return jnp.minimum(jnp.maximum(result, -bound), bound).astype(kind)


def setup_inputs(seed: int = 0) -> dict:
    splits = jax.random.split(jax.random.key(seed), 11)
    return {
        "velocity": normal_values(splits[0], (CIN, NX, NY * NZ), 1.0, 6.0, ((1, 64), (2, 8))),
        "cotangent": normal_values(splits[1], (CIN, NX, NY * NZ), 1.0, 6.0, ((1, 64), (2, 8))),
        "kernel_one": normal_values(splits[2], (TAPS, C1, CIN), (TAPS * CIN) ** -0.5, 0.625),
        "kernel_two": normal_values(splits[3], (TAPS, C2, C1), (TAPS * C1) ** -0.5, 0.3125),
        "kernel_three": normal_values(splits[4], (TAPS, C3, C2), (TAPS * C2) ** -0.5, 0.21875),
        "kernel_four": normal_values(splits[5], (TAPS, C4, C3), (TAPS * C3) ** -0.5, 0.15625),
        "lift_four": normal_values(splits[6], (C3, C4), C4 ** -0.5, 0.5),
        "lift_three": normal_values(splits[7], (C2, C3), C3 ** -0.5, 0.75),
        "lift_two": normal_values(splits[8], (C1, C2), C2 ** -0.5, 1.0),
        "head": normal_values(splits[9], (CIN, C1), C1 ** -0.5, 1.5),
    }


def silu_slope(pre):
    sigma = jax.nn.sigmoid(pre)
    return sigma * (1.0 + pre * (1.0 - sigma))


def pad_depth(field):
    return jnp.pad(field, ((0, 0), (0, 0), (0, 0), (1, 1)))


def pad_side(field):
    return pad_depth(jnp.pad(field, ((0, 0), (0, 0), (1, 1), (0, 0)), mode="wrap"))


def pad_periodic(field):
    return pad_side(jnp.pad(field, ((0, 0), (1, 1), (0, 0), (0, 0)), mode="wrap"))


def window_at(padded, offset, extent):
    first, second, third = offset // 9, offset // 3 % 3, offset % 3
    piece = lax.slice(padded, (0, first, second, third), (padded.shape[0], first + extent[0], second + extent[1], third + extent[2]))
    return piece.reshape(padded.shape[0], -1)


def correlate(padded, kernel, extent):
    total = jnp.zeros((kernel.shape[1], extent[0] * extent[1] * extent[2]), jnp.float32)
    for offset in range(TAPS):
        total = total + jnp.dot(kernel[offset], window_at(padded, offset, extent), preferred_element_type=jnp.float32)
    return total.reshape((kernel.shape[1], extent[0], extent[1], extent[2]))


def kernel_slope(padded, delta):
    extent = delta.shape[1:]
    flat = delta.reshape(delta.shape[0], -1)
    rows = [lax.dot_general(flat, window_at(padded, offset, extent), (((1,), (1,)), ((), ())), preferred_element_type=jnp.float32) for offset in range(TAPS)]
    return jnp.stack(rows)


def reflect(kernel):
    return jnp.transpose(kernel[::-1], (0, 2, 1))


def cells_dot(left, right):
    return lax.dot_general(left.reshape(left.shape[0], -1), right.reshape(right.shape[0], -1), (((1,), (1,)), ((), ())), preferred_element_type=jnp.float32)


def pool_sum(field):
    chans, first, second, third = field.shape
    return field.astype(jnp.float32).reshape(chans, first // 2, 2, second // 2, 2, third // 2, 2).sum(axis=(2, 4, 6))


def shrink(field):
    return (pool_sum(field) * 0.125).astype(jnp.bfloat16)


def enlarge(field):
    return jnp.repeat(jnp.repeat(jnp.repeat(field, 2, axis=1), 2, axis=2), 2, axis=3)


def project(weight, field):
    chans, first, second, third = field.shape
    return jnp.dot(weight, field.reshape(chans, -1), preferred_element_type=jnp.float32).reshape(weight.shape[0], first, second, third)


def encode(padded, kernel, extent):
    pre = correlate(padded, kernel, extent)
    return pre, jax.nn.silu(pre).astype(jnp.bfloat16)


def reference(velocity, cotangent, kernel_one, kernel_two, kernel_three, kernel_four, lift_four, lift_three, lift_two, head):
    field = velocity.reshape(CIN, NX, NY, NZ)
    padded_fine = pad_periodic(field)
    pre_fine, act_fine = encode(padded_fine, kernel_one, field.shape[1:])
    pooled_mid = shrink(act_fine)
    padded_mid = pad_periodic(pooled_mid)
    pre_mid, act_mid = encode(padded_mid, kernel_two, pooled_mid.shape[1:])
    pooled_coarse = shrink(act_mid)
    padded_coarse = pad_periodic(pooled_coarse)
    pre_coarse, act_coarse = encode(padded_coarse, kernel_three, pooled_coarse.shape[1:])
    pooled_bottom = shrink(act_coarse)
    padded_bottom = pad_periodic(pooled_bottom)
    pre_bottom, act_bottom = encode(padded_bottom, kernel_four, pooled_bottom.shape[1:])
    skip_coarse = (act_coarse + enlarge(project(lift_four, act_bottom))).astype(jnp.bfloat16)
    skip_mid = (act_mid + enlarge(project(lift_three, skip_coarse))).astype(jnp.bfloat16)
    skip_fine = (act_fine + enlarge(project(lift_two, skip_mid))).astype(jnp.bfloat16)
    prediction = project(head, skip_fine)

    incoming = cotangent.reshape(CIN, NX, NY, NZ)
    grad_head = cells_dot(incoming, skip_fine)
    back_fine = project(head.T, incoming).astype(jnp.bfloat16)
    carry_mid = pool_sum(back_fine).astype(jnp.bfloat16)
    grad_lift_two = cells_dot(carry_mid, skip_mid)
    back_mid = project(lift_two.T, carry_mid).astype(jnp.bfloat16)
    carry_coarse = pool_sum(back_mid).astype(jnp.bfloat16)
    grad_lift_three = cells_dot(carry_coarse, skip_coarse)
    back_coarse = project(lift_three.T, carry_coarse).astype(jnp.bfloat16)
    carry_bottom = pool_sum(back_coarse).astype(jnp.bfloat16)
    grad_lift_four = cells_dot(carry_bottom, act_bottom)
    slope_bottom = project(lift_four.T, carry_bottom)

    delta_bottom = (slope_bottom * silu_slope(pre_bottom)).astype(jnp.bfloat16)
    grad_kernel_four = kernel_slope(padded_bottom, delta_bottom)
    return_bottom = correlate(pad_periodic(delta_bottom), reflect(kernel_four), delta_bottom.shape[1:])
    slope_coarse = back_coarse + enlarge(return_bottom) * 0.125
    delta_coarse = (slope_coarse * silu_slope(pre_coarse)).astype(jnp.bfloat16)
    grad_kernel_three = kernel_slope(padded_coarse, delta_coarse)
    return_coarse = correlate(pad_periodic(delta_coarse), reflect(kernel_three), delta_coarse.shape[1:])
    slope_mid = back_mid + enlarge(return_coarse) * 0.125
    delta_mid = (slope_mid * silu_slope(pre_mid)).astype(jnp.bfloat16)
    grad_kernel_two = kernel_slope(padded_mid, delta_mid)
    return_mid = correlate(pad_periodic(delta_mid), reflect(kernel_two), delta_mid.shape[1:])
    slope_fine = back_fine + enlarge(return_mid) * 0.125
    delta_fine = (slope_fine * silu_slope(pre_fine)).astype(jnp.bfloat16)
    grad_kernel_one = kernel_slope(padded_fine, delta_fine)
    grad_velocity = correlate(pad_periodic(delta_fine), reflect(kernel_one), delta_fine.shape[1:])

    scale = float(NX * NY * NZ) ** -0.5
    return (prediction.reshape(CIN, NX, NY * NZ), grad_velocity.reshape(CIN, NX, NY * NZ),
            grad_kernel_one * scale, grad_kernel_two * scale, grad_kernel_three * scale, grad_kernel_four * scale,
            grad_lift_four * scale, grad_lift_three * scale, grad_lift_two * scale, grad_head * scale)
```

```python
import jax
import jax.numpy as jnp
import numpy as np
from jax import lax
from jax.experimental import pallas as pl
from jax.experimental.pallas import tpu as pltpu
from jax.sharding import PartitionSpec as P

BF = jnp.bfloat16
F32 = jnp.float32
NZ = 16
LINES = 9
PIECE = 40
SHARE = 8 * PIECE
PACK = 8 * SHARE


def mm(a, b):
    return lax.dot_general(a, b, (((1,), (0,)), ((), ())), preferred_element_type=F32)


def mm_nt(a, b):
    return lax.dot_general(a, b, (((1,), (1,)), ((), ())), preferred_element_type=F32)


def mm_tn(a, b):
    return lax.dot_general(a, b, (((0,), (0,)), ((), ())), preferred_element_type=F32)


def halves(x):
    high = x.astype(BF)
    return high, (x - high.astype(F32)).astype(BF)


def mm2(x, e):
    high, low = halves(x)
    return mm(high, e) + mm(low, e)


def iota(shape, axis):
    return lax.broadcasted_iota(jnp.int32, shape, axis)


def log2(n):
    return int(n).bit_length() - 1


def one_hot(mask):
    return jnp.where(mask, 1.0, 0.0).astype(BF)


def pool_matrix(chans):
    row, col = iota((256, 128), 0), iota((256, 128), 1)
    shift = log2(chans)
    same = (row & (chans - 1)) == (col & (chans - 1))
    return one_hot(same & ((row >> (shift + 1)) == (col >> shift)))


def tile_matrix(chans, lanes):
    return one_hot(iota((chans, lanes), 0) == (iota((chans, lanes), 1) & (chans - 1)))


def fold_matrix(rows, chans, lead):
    row, col = iota((rows, 128), 0), iota((rows, 128), 1)
    return one_hot((row & (chans - 1)) + lead == col)


def shift_y(v, count, step):
    rows = v.shape[0]
    out = pltpu.roll(v, (-step) % rows, 0)
    if rows == count:
        return out
    if step == 1:
        other, edge = pltpu.roll(v, count - 1, 0), count - 1
    else:
        other, edge = pltpu.roll(v, rows - (count - 1), 0), 0
    spot = iota(v.shape, 0) & (count - 1)
    return jnp.where(spot == edge, other, out)


def silu_of(pre):
    half = 0.5 * pre
    return half + half * jnp.tanh(half)


def slope_of(pre):
    half = 0.5 * pre
    bend = jnp.tanh(half)
    return (0.5 + 0.5 * bend) * (1.0 + half * (1.0 - bend))


def prep_kernel(vel_ref, cot_ref, place_ref, out_ref):
    row, col = iota((64, 128), 0), iota((64, 128), 1)
    mask = (row & 7) == (col >> 4)
    spread = one_hot((iota((64, 8), 0) >> 3) == iota((64, 8), 1))
    total = jnp.zeros((64, 128), F32)
    for part, ref in ((0, vel_ref), (1, cot_ref)):
        for chan in range(3):
            wide = mm(spread, ref[chan])
            kept = jnp.where(mask, wide, 0.0).astype(BF)
            total = total + mm(kept, place_ref[part * 3 + chan])
    last = total[48:64]
    spare = iota((16, 128), 1) >= 96
    for g in range(3):
        moved = pltpu.roll(last, 96 - 32 * g, 1)
        out_ref[g * 16:(g + 1) * 16, :] = jnp.where(
            spare, moved, total[g * 16:(g + 1) * 16]
        ).astype(BF)


def build_kernel(
    k1_ref,
    k2_ref,
    k3_ref,
    k4_ref,
    l4_ref,
    l3_ref,
    l2_ref,
    head_ref,
    band_ref,
    base_ref,
    rowrep_ref,
    headmask_ref,
    t1,
    t2,
    t3,
    t4,
    f4,
    f3,
    f2,
    hp,
    b4,
    b3,
    b2,
    small,
):
    def build(kernel_ref, t_ref, outs, ins):
        planes = 128 // ins
        rep = mm(kernel_ref[...], tile_matrix(outs, 256))
        kout = iota((ins, 256), 1) >> log2(outs)
        for ab in range(9):
            a, b = ab // 3, ab % 3
            taps = [rep[(ab * 3 + c) * ins:(ab * 3 + c + 1) * ins] for c in range(3)]
            for k in range(planes):
                block = jnp.zeros((ins, 256), F32)
                for c in range(3):
                    if 0 <= k - c + 1 < planes:
                        block = jnp.where(kout == k - c + 1, taps[c], block)
                start = b * 128 + k * ins
                t_ref[a, start:start + ins, :] = block.astype(BF)

    build(k2_ref, t2, 32, 16)
    build(k3_ref, t3, 64, 32)
    build(k4_ref, t4, 128, 64)
    small[...] = jnp.zeros(small.shape, F32)
    for c in range(3):
        small[c * 32:c * 32 + 27, :] = mm_tn(k1_ref[c], tile_matrix(16, 256))
    rep1 = small[...].astype(BF)
    base = base_ref[...]
    band = band_ref[...]
    for a in range(3):
        block = jnp.zeros((256, 256), F32)
        for c in range(3):
            block = jnp.where(band == c, mm(one_hot(base == 9 * a + c), rep1), block)
        t1[a] = block.astype(BF)

    def lift(lift_ref, f_ref, b_ref, coarse):
        fine, chans = lift_ref.shape
        rep = mm(lift_ref[...], tile_matrix(chans, 256))
        kin = iota((fine, 256), 1) >> log2(chans)
        for k in range(2 * coarse):
            f_ref[k * fine:(k + 1) * fine, :] = jnp.where(kin == k // 2, rep, 0.0).astype(BF)
        for k in range(coarse):
            b_ref[k * fine:(k + 1) * fine, :] = jnp.where(kin == k, rep, 0.0).astype(BF)

    lift(l4_ref, f4, b4, 2)
    lift(l3_ref, f3, b3, 4)
    lift(l2_ref, f2, b2, 8)
    small[0:16, 0:128] = jnp.zeros((16, 128), F32)
    small[0:3, 0:16] = head_ref[...].astype(F32)
    tileh = one_hot(iota((128, 256), 0) == (iota((128, 256), 1) & 15))
    reph = mm(small[0:16, 0:128].astype(BF), tileh).astype(BF)
    hp[...] = (mm(rowrep_ref[...], reph) * headmask_ref[...]).astype(BF)


def main_kernel(
    where_ref,
    own_ref,
    tiles_ref,
    t1,
    t2,
    t3,
    t4,
    f4,
    f3,
    f2,
    hp,
    b4,
    b3,
    b2,
    band_ref,
    pick_ref,
    rowrep_ref,
    headmask_ref,
    unplace_ref,
    pred_ref,
    gradv_ref,
    share_ref,
    xt,
    xc,
    v3,
    pre1,
    act1,
    pre2,
    act2,
    pre3,
    act3,
    p32,
    p33,
    p34,
    skip1,
    carry2,
    carry3,
    back2,
    back3,
    d1,
    d2,
    d3,
    d4,
    ret2,
    tmp,
    ups_a,
    ups_b,
    line,
    pack,
):
    own_part = where_ref[0]
    lane = iota((1, 128), 1)
    band = band_ref[...]

    pool1, pool2, pool3 = pool_matrix(16), pool_matrix(32), pool_matrix(64)

    def rows(start, count, unit):
        return pl.ds(pl.multiple_of(start, unit), count)

    v3[0:64, :] = jnp.zeros((64, 256), BF)
    v3[73 * 64:74 * 64, :] = jnp.zeros((64, 256), BF)

    def arrange(source, number):
        for n in range(8):
            tile = source(n).astype(F32)
            last = jnp.zeros((16, 128), F32)
            for g in range(3):
                moved = pltpu.roll(tile[g * 16:(g + 1) * 16], 32 * (g + 1), 1)
                last = jnp.where((lane >= 32 * g) & (lane < 32 * g + 32), moved, last)
            for i in range(8):
                piece = tile[i * 8:i * 8 + 8] if i < 6 else last[(i - 6) * 8:(i - 5) * 8]
                xt[i * 64 + n * 8:i * 64 + n * 8 + 8, :] = piece
        for i in range(8):
            row = xt[i * 64:(i + 1) * 64, :]
            xc[rows((number * 8 + i) * 64, 64, 64), :] = row.astype(BF)
            vel = jnp.where(lane < 48, row, 0.0)
            low = pltpu.roll(vel, 1, 0) + pltpu.roll(vel, 48, 1)
            high = pltpu.roll(vel, 63, 0)
            spot = rows((number * 8 + i + 1) * 64, 64, 64)
            v3[spot, 0:128] = low.astype(BF)
            v3[spot, 128:256] = high.astype(BF)

    def arrange_far(step, _):
        arrange(lambda n: tiles_ref[step, n], where_ref[1 + step])
        return 0

    arrange(lambda n: own_ref[n], 4)
    lax.fori_loop(0, 8, arrange_far, 0)

    def pooled(field, matrix, count):
        flat = mm(field, matrix)
        pairs = field.shape[0] // (2 * count)
        for i in range(pairs):
            tmp[i * count:(i + 1) * count, :] = (
                flat[2 * i * count:(2 * i + 1) * count] + flat[(2 * i + 1) * count:(2 * i + 2) * count]
            )
        n = pairs * count // 2
        return tmp[pl.ds(0, n, stride=2), :] + tmp[pl.ds(1, n, stride=2), :]

    def enlarged(field, count):
        n = field.shape[0]
        for half, ref in ((0, ups_a), (1, ups_b)):
            piece = field[:, half * 128:(half + 1) * 128]
            ref[pl.ds(0, n, stride=2), :] = piece
            ref[pl.ds(1, n, stride=2), :] = piece
        big = jnp.concatenate([ups_a[0:2 * n, :], ups_b[0:2 * n, :]], axis=1)
        wide = 2 * count
        parts = []
        for i in range(n // count):
            piece = big[i * wide:(i + 1) * wide]
            parts += [piece, piece]
        return jnp.concatenate(parts, axis=0)

    def put3(ref, start, unit, field, count):
        spot = rows(start, field.shape[0], unit)
        kind = ref.dtype
        ref[spot, 0:128] = shift_y(field, count, -1).astype(kind)
        ref[spot, 128:256] = field.astype(kind)
        ref[spot, 256:384] = shift_y(field, count, 1).astype(kind)

    def fine_forward(step, _):
        start = step * 512
        pre = mm(v3[rows(start, 512, 64), :], t1[0])
        for a in (1, 2):
            pre = pre + mm(v3[rows(start + a * 64, 512, 64), :], t1[a])
        pre1[rows(start, 512, 512), :] = pre
        act = silu_of(pre).astype(BF)
        act1[rows(start, 512, 512), :] = act
        half = (pooled(act, pool1, 64) * 0.125).astype(BF).astype(F32)
        put3(p32, step * 128, 32, half, 32)
        return 0

    lax.fori_loop(0, 9, fine_forward, 0)

    def mid_forward(step, _):
        start = (2 + step * 8) * 32
        pre = mm(p32[rows(start - 32, 256, 32), :], t2[0])
        for a in (1, 2):
            pre = pre + mm(p32[rows(start + (a - 1) * 32, 256, 32), :], t2[a])
        pre2[rows(start, 256, 32), :] = pre
        act = silu_of(pre).astype(BF)
        act2[rows(start, 256, 32), :] = act
        half = (pooled(act, pool2, 32) * 0.125).astype(BF).astype(F32)
        put3(p33, (1 + step * 4) * 16, 16, half, 16)
        return 0

    lax.fori_loop(0, 4, mid_forward, 0)

    pre = mm(p33[16:240, :], t3[0])
    for a in (1, 2):
        pre = pre + mm(p33[(1 + a) * 16:(1 + a) * 16 + 224, :], t3[a])
    pre3[...] = pre
    act = silu_of(pre).astype(BF)
    act3[...] = act
    half = (pooled(act, pool3, 16) * 0.125).astype(BF).astype(F32)
    put3(p34, 8, 8, half, 8)

    pre4 = mm(p34[8:48, :].astype(BF), t4[0])
    for a in (1, 2):
        pre4 = pre4 + mm(p34[(1 + a) * 8:(1 + a) * 8 + 40, :].astype(BF), t4[a])
    act4 = silu_of(pre4)[16:24].astype(BF)

    skip3 = (act3[96:128, :].astype(F32) + enlarged(mm_nt(act4, f4[...]), 8)).astype(BF)
    skip2 = (act2[512:640, :].astype(F32) + enlarged(mm_nt(skip3, f3[...]), 16)).astype(BF)
    up2 = mm_nt(skip2, f2[...])
    for half in range(2):
        base = act1[2048 + half * 256:2304 + half * 256, :].astype(F32)
        up = enlarged(up2[half * 64:(half + 1) * 64], 32)
        skip1[half * 256:(half + 1) * 256, :] = (base + up).astype(BF)
    gh = mm_tn(xc[2048:2560, :], skip1[...])

    def fine_carry(step, _):
        back = mm(xc[rows((16 + step * 8) * 64, 512, 512), :], hp[...]).astype(BF)
        carry2[rows((8 + step * 4) * 32, 128, 128), :] = pooled(back, pool1, 64).astype(BF)
        return 0

    lax.fori_loop(0, 5, fine_carry, 0)

    for step in range(5):
        start = (8 + step * 4) * 32
        back = mm(carry2[start:start + 128, :], b2[...]).astype(BF)
        back2[start:start + 128, :] = back
        carry3[step * 32:(step + 1) * 32, :] = pooled(back, pool2, 32).astype(BF)
    back = mm(carry3[...], b3[...]).astype(BF)
    back3[...] = back
    carry4 = pooled(back, pool3, 16)

    gl2 = mm_tn(carry2[512:640, :], skip2)
    gl3 = mm_tn(carry3[64:96, :], skip3)
    gl4 = mm_tn(carry4[16:24].astype(BF), act4)

    delta4 = (mm(carry4.astype(BF), b4[...]) * slope_of(pre4)).astype(BF).astype(F32)
    d4[...] = delta4
    own4 = delta4[16:24].astype(BF)

    def returned(total, count):
        return (
            shift_y(total[:, 0:128], count, 1)
            + total[:, 128:256]
            + shift_y(total[:, 256:384], count, -1)
        )

    total = mm_nt(d4[16:40, :].astype(BF), t4[0])
    for a in (1, 2):
        total = total + mm_nt(d4[(2 - a) * 8:(2 - a) * 8 + 24, :].astype(BF), t4[a])
    ret4 = returned(total, 8)

    def spread_up(field, matrix, count):
        high, low = halves(field * 0.125)
        return enlarged(mm_nt(high, matrix) + mm_nt(low, matrix), count)

    slope = back3[32:128, :].astype(F32) + spread_up(ret4, pool3, 8)
    d3[...] = (slope * slope_of(pre3[64:160, :])).astype(BF)
    total = mm_nt(d3[32:96, :], t3[0])
    for a in (1, 2):
        total = total + mm_nt(d3[(2 - a) * 16:(2 - a) * 16 + 64, :], t3[a])
    ret3 = returned(total, 16)

    slope = back2[14 * 32:22 * 32, :].astype(F32) + spread_up(ret3, pool2, 16)
    d2[...] = (slope * slope_of(pre2[14 * 32:22 * 32, :])).astype(BF)
    total = mm_nt(d2[64:256, :], t2[0])
    for a in (1, 2):
        total = total + mm_nt(d2[(2 - a) * 32:(2 - a) * 32 + 192, :], t2[a])
    ret2[...] = returned(total, 32)

    for step in range(3):
        spot = slice((30 + step * 4) * 64, (34 + step * 4) * 64)
        up = spread_up(ret2[step * 64:(step + 1) * 64, :], pool1, 32)
        back = mm(xc[spot, :], hp[...]).astype(BF).astype(F32)
        d1[step * 256:(step + 1) * 256, :] = ((back + up) * slope_of(pre1[spot, :])).astype(BF)

    guess = mm_nt(skip1[...], hp[...])
    total = mm_nt(d1[192:704, :], t1[0])
    for a in (1, 2):
        total = total + mm_nt(d1[(3 - a) * 64:(3 - a) * 64 + 512, :], t1[a])
    low, high = total[:, 0:128], total[:, 128:256]
    grad = shift_y(low, 64, 1) + pltpu.roll(low, 80, 1) + shift_y(high, 64, -1)
    line[...] = jnp.where(lane < 48, grad, guess)
    pieces = [line[rows(i * 64 + own_part * 8, 8, 8), :] for i in range(8)]
    own = jnp.concatenate(pieces, axis=0)
    first, rest = halves(own)
    second, third = halves(own - first.astype(F32))
    mask = (iota((64, 128), 0) & 7) == (iota((64, 128), 1) >> 4)
    for part, ref in ((0, gradv_ref), (1, pred_ref)):
        for chan in range(3):
            matrix = unplace_ref[part * 3 + chan]
            full = mm(first, matrix) + mm(second, matrix) + mm(third, matrix)
            full = jnp.where(mask, full, 0.0).reshape(8, 8, 128)
            ref[chan] = jnp.sum(full, axis=1)

    pack[1728:PACK, :] = jnp.zeros((PACK - 1728, 128), F32)

    def fold_taps(product, outs, ins, a, b):
        planes = 128 // ins
        kout = iota((ins, 256), 1) >> log2(outs)
        sums = [jnp.zeros((ins, 256), F32) for _ in range(3)]
        for k in range(planes):
            block = product[b * 128 + k * ins:b * 128 + (k + 1) * ins]
            for c in range(3):
                if 0 <= k - c + 1 < planes:
                    sums[c] = sums[c] + jnp.where(kout == k - c + 1, block, 0.0)
        joined = jnp.concatenate(sums, axis=0)
        joined = joined[:, 0:128] + joined[:, 128:256]
        width = outs
        while width < 128:
            joined = joined + pltpu.roll(joined, 128 - width, 1)
            width *= 2
        return joined

    fold4, fold2 = fold_matrix(256, 128, 0), fold_matrix(256, 32, 64)
    for a in range(3):
        product = mm_tn(p34[(3 + a) * 8:(4 + a) * 8, :].astype(BF), own4)
        for b in range(3):
            start = (a * 3 + b) * 192
            pack[start:start + 192, :] = fold_taps(product, 128, 64, a, b)
    for a in range(3):
        product = mm_tn(p33[(7 + a) * 16:(9 + a) * 16, :], d3[32:64, :])
        for b in range(3):
            part = fold_taps(product, 64, 32, a, b)
            left = jnp.where(lane < 64, part, 0.0)
            start = 1728 + (a * 3 + b) * 96
            if a * 3 + b < 8:
                pack[start:start + 96, :] = left
            else:
                pack[2496:2560, :] = left[0:64]
                pack[2352:2384, :] += jnp.where(lane >= 64, part[64:96], 0.0)
    for a in range(3):
        product = mm_tn(p32[(15 + a) * 32:(19 + a) * 32, :], d2[64:192, :])
        for b in range(3):
            part = fold_taps(product, 32, 16, a, b)
            start = 1728 + (a * 3 + b) * 48
            pack[start:start + 48, :] += jnp.where((lane >= 64) & (lane < 96), part, 0.0)
    fold1 = fold_matrix(256, 16, 96)
    for a in range(3):
        product = mm_tn(v3[(32 + a) * 64:(40 + a) * 64, :], d1[128:640, :])
        for c in range(3):
            high, low = halves(jnp.where(band == c, product, 0.0))
            sums = mm_tn(pick_ref[...], high) + mm_tn(pick_ref[...], low)
            start = 1728 + (a * 3 + c) * 16
            pack[start:start + 16, :] += mm2(sums, fold1)

    def fold_lift(product, fine, chans, matrix):
        kin = iota((fine, 256), 1) >> log2(chans)
        total = jnp.zeros((fine, 256), F32)
        for k in range(256 // chans):
            total = total + jnp.where(kin == k, product[k * fine:(k + 1) * fine], 0.0)
        return mm2(total, matrix)

    pack[2160:2192, :] += fold_lift(gl3, 32, 64, fold_matrix(256, 64, 64))
    pack[2192:2208, :] += fold_lift(gl2, 16, 32, fold2)
    high, low = halves(gh * headmask_ref[...])
    heads = mm_tn(rowrep_ref[...], high) + mm_tn(rowrep_ref[...], low)
    pack[2208:2224, :] += mm2(heads, fold_matrix(256, 16, 64))
    lift4 = fold_lift(gl4, 64, 128, fold4)
    pack[2224:2288, :] += jnp.where(lane >= 64, pltpu.roll(lift4, 64, 1), 0.0)
    pack[2288:2352, :] += jnp.where(lane >= 64, lift4, 0.0)
    share_ref[...] = pack[rows(own_part * SHARE, SHARE, SHARE), :].astype(BF)


def unpack_kernel(full_ref, order_ref, g1_ref, g2_ref, g3_ref, g4_ref, l4_ref, l3_ref, l2_ref, head_ref):
    scale = float(512 * 64 * 16) ** -0.5

    def left(start, count):
        return full_ref[start:start + count, :].astype(F32) * scale

    def right(start, count):
        return pltpu.roll(left(start, count), 64, 1)

    g4_ref[...] = left(0, 1728)
    g3_ref[0:832, :] = left(1728, 832)[:, 0:64]
    g3_ref[832:864, :] = right(2352, 32)[:, 0:64]
    g2_ref[...] = right(1728, 432)[:, 0:32]
    for c in range(3):
        turned = mm_tn(full_ref[1728:1872, :], order_ref[c]) * scale
        g1_ref[c] = turned[96:112, 0:27]
    l3_ref[...] = right(2160, 32)[:, 0:64]
    l2_ref[...] = right(2192, 16)[:, 0:32]
    head_ref[...] = right(2208, 16)[0:3, 0:16]
    l4_ref[:, 0:64] = right(2224, 64)[:, 0:64]
    l4_ref[:, 64:128] = left(2288, 64)[:, 64:128]


def constants():
    lanes = np.arange(128)
    kin = np.where(lanes < 96, (lanes % 48) // 3, -9)
    chan = np.where(lanes < 96, lanes % 3, -9)
    second = (lanes >= 48) & (lanes < 96)
    rowrep = (second[:, None] & (chan[:, None] == np.arange(16)[None, :])).astype(np.float32)
    headmask = (second[:, None] & (kin[:, None] == (np.arange(256) // 16)[None, :])).astype(np.float32)
    place = np.zeros((6, 128, 128), np.float32)
    for part in range(2):
        for c in range(3):
            for row in range(128):
                place[part * 3 + c, row, part * 48 + (row % 16) * 3 + c] = 1.0
    unplace = place.transpose(0, 2, 1)
    pick = np.zeros((256, 16), np.float32)
    band = np.full((256, 256), -9, np.int32)
    base = np.full((256, 128), -99, np.int32)
    order = np.zeros((3, 144, 128), np.float32)
    for b, lead in enumerate((0, 48, 128)):
        for k in range(16):
            for c in range(3):
                pick[lead + k * 3 + c, b * 3 + c] = 1.0
                band[lead + k * 3 + c] = k - np.arange(256) // 16 + 1
                base[lead + k * 3 + c] = lanes - 32 * c - 3 * b
    for tap in range(27):
        a, b, step = tap // 9, tap // 3 % 3, tap % 3
        for c in range(3):
            order[c, (a * 3 + step) * 16 + b * 3 + c, tap] = 1.0
    return order, base, band, pick, rowrep, headmask, place, unplace


def run_build(weights, interpret=False):
    _, base, band, _, rowrep, headmask, _, _ = constants()
    k1, k2, k3, k4, l4, l3, l2, head = weights
    shapes = ((3, 256, 256),) + ((3, 384, 256),) * 3 + ((256, 256),) * 3 + ((128, 256),) * 4
    return pl.pallas_call(
        build_kernel,
        out_shape=tuple(jax.ShapeDtypeStruct(shape, BF) for shape in shapes),
        scratch_shapes=[pltpu.VMEM((128, 256), F32)],
        compiler_params=pltpu.CompilerParams(vmem_limit_bytes=24 * 1024 * 1024),
        interpret=interpret,
    )(
        k1.transpose(2, 1, 0),
        k2.transpose(0, 2, 1).reshape(432, 32),
        k3.transpose(0, 2, 1).reshape(864, 64),
        k4.transpose(0, 2, 1).reshape(1728, 128),
        l4,
        l3,
        l2,
        head,
        jnp.asarray(band),
        jnp.asarray(base),
        jnp.asarray(rowrep, BF),
        jnp.asarray(headmask, F32),
    )


def run_main(where, own, tiles, matrices, interpret=False):
    _, _, band, pick, rowrep, headmask, _, unplace = constants()
    vm = pl.BlockSpec(memory_space=pltpu.VMEM)

    def buf(shape, kind=BF):
        return pltpu.VMEM(shape, kind)

    scratch = [
        buf((512, 128), F32),
        buf((72 * 64, 128)),
        buf((74 * 64, 256)),
        buf((72 * 64, 256), F32),
        buf((72 * 64, 256)),
        buf((36 * 32, 256), F32),
        buf((36 * 32, 256)),
        buf((224, 256), F32),
        buf((224, 256)),
        buf((36 * 32, 384)),
        buf((18 * 16, 384)),
        buf((9 * 8, 384), F32),
        buf((512, 256)),
        buf((36 * 32, 128)),
        buf((160, 128)),
        buf((36 * 32, 256)),
        buf((160, 256)),
        buf((768, 256)),
        buf((256, 256)),
        buf((96, 256)),
        buf((40, 256), F32),
        buf((192, 128), F32),
        buf((256, 128), F32),
        buf((128, 128), F32),
        buf((128, 128), F32),
        buf((512, 128), F32),
        buf((PACK, 128), F32),
    ]
    return pl.pallas_call(
        main_kernel,
        out_shape=(
            jax.ShapeDtypeStruct((3, 8, 128), F32),
            jax.ShapeDtypeStruct((3, 8, 128), F32),
            jax.ShapeDtypeStruct((SHARE, 128), BF),
        ),
        in_specs=[pl.BlockSpec(memory_space=pltpu.SMEM)] + [vm] * 18,
        out_specs=(vm, vm, vm),
        scratch_shapes=scratch,
        compiler_params=pltpu.CompilerParams(vmem_limit_bytes=44 * 1024 * 1024),
        interpret=interpret,
    )(
        where,
        own,
        tiles,
        *matrices,
        jnp.asarray(band),
        jnp.asarray(pick, BF),
        jnp.asarray(rowrep, BF),
        jnp.asarray(headmask, F32),
        jnp.asarray(unplace, BF),
    )


def run_prep(velocity, cotangent, interpret=False):
    place = constants()[6]
    return pl.pallas_call(
        prep_kernel,
        out_shape=jax.ShapeDtypeStruct((48, 128), BF),
        interpret=interpret,
    )(velocity, cotangent, jnp.asarray(place, BF))


def unpack(full, interpret=False):
    order = constants()[0]
    shapes = ((3, 16, 27), (432, 32), (864, 64), (1728, 128), (64, 128), (32, 64), (16, 32), (3, 16))
    g1, g2, g3, g4, l4, l3, l2, head = pl.pallas_call(
        unpack_kernel,
        out_shape=tuple(jax.ShapeDtypeStruct(shape, F32) for shape in shapes),
        interpret=interpret,
    )(full, jnp.asarray(order, BF))
    return (
        g1.transpose(2, 1, 0),
        g2.reshape(27, 16, 32).transpose(0, 2, 1),
        g3.reshape(27, 32, 64).transpose(0, 2, 1),
        g4.reshape(27, 64, 128).transpose(0, 2, 1),
        l4,
        l3,
        l2,
        head,
    )


FAR = (4, -1, -4, 1, 3, -2, -3, 2)
GROUP_Y = [[8 * z + y for y in range(8)] for z in range(8)]
GROUP_Z = [[8 * z + y for z in range(8)] for y in range(8)]


def exchange(x, groups):
    return lax.all_to_all(x, "wide", 0, 0, axis_index_groups=groups, tiled=True)


def local(velocity, cotangent, *weights):
    where = jnp.stack([lax.axis_index("narrow")] + [4 + step for step in FAR]).astype(jnp.int32)
    tile = run_prep(velocity, cotangent)
    own = lax.all_gather(tile, "narrow", axis=0)
    routes = [((w + FAR[n]) % 64 * 8 + n, w * 8 + n) for w in range(64) for n in range(8)]
    far = lax.ppermute(own, ("wide", "narrow"), routes)
    tiles = lax.all_gather(far, "narrow", axis=0)
    prediction, grad_velocity, share = run_main(where, own, tiles, run_build(weights))
    pieces = exchange(share.reshape(8, PIECE, 128), GROUP_Y)
    partial = pieces.astype(F32).sum(axis=0).astype(BF)
    pieces = exchange(jnp.broadcast_to(partial, (8, PIECE, 128)), GROUP_Z)
    total = pieces.astype(F32).sum(axis=0).astype(BF)
    whole = exchange(jnp.broadcast_to(total, (8, PIECE, 128)), GROUP_Y).reshape(SHARE, 128)
    full = lax.all_gather(whole, "narrow", axis=0).reshape(PACK, 128)
    return (prediction, grad_velocity) + unpack(full)


def solution(mesh):
    split = P(None, "wide", "narrow")
    return jax.shard_map(
        local,
        mesh=mesh,
        in_specs=(split, split) + (P(),) * 8,
        out_specs=(split, split) + (P(),) * 8,
        check_vma=False,
    )
```

```python
import jax
import jax.numpy as jnp
import numpy as np
from jax import lax
from jax.experimental import pallas as pl
from jax.experimental.pallas import tpu as pltpu
from jax.sharding import PartitionSpec as P

BF = jnp.bfloat16
F32 = jnp.float32
NZ = 16
LINES = 9
PIECE = 40
SHARE = 8 * PIECE
PACK = 8 * SHARE


def mm(a, b):
    return lax.dot_general(a, b, (((1,), (0,)), ((), ())), preferred_element_type=F32)


def mm_nt(a, b):
    return lax.dot_general(a, b, (((1,), (1,)), ((), ())), preferred_element_type=F32)


def mm_tn(a, b):
    return lax.dot_general(a, b, (((0,), (0,)), ((), ())), preferred_element_type=F32)


def halves(x):
    high = x.astype(BF)
    return high, (x - high.astype(F32)).astype(BF)


def mm2(x, e):
    high, low = halves(x)
    return mm(high, e) + mm(low, e)


def iota(shape, axis):
    return lax.broadcasted_iota(jnp.int32, shape, axis)


def log2(n):
    return int(n).bit_length() - 1


def one_hot(mask):
    return jnp.where(mask, 1.0, 0.0).astype(BF)


def pool_matrix(chans):
    row, col = iota((256, 128), 0), iota((256, 128), 1)
    shift = log2(chans)
    same = (row & (chans - 1)) == (col & (chans - 1))
    return one_hot(same & ((row >> (shift + 1)) == (col >> shift)))


def tile_matrix(chans, lanes):
    return one_hot(iota((chans, lanes), 0) == (iota((chans, lanes), 1) & (chans - 1)))


def fold_matrix(rows, chans, lead):
    row, col = iota((rows, 128), 0), iota((rows, 128), 1)
    return one_hot((row & (chans - 1)) + lead == col)


def packed(shape):
    row = iota(shape, 0)
    b = jnp.where(row < 48, 0, jnp.where(row < 96, 1, 2))
    left = row - jnp.where(row < 48, 0, jnp.where(row < 96, 48, 128))
    kin = (left * 43) >> 7
    valid = (row < 96) | ((row >= 128) & (row < 176))
    return valid, b, kin, left - 3 * kin


def band_matrix():
    valid, _, kin, _ = packed((256, 256))
    return jnp.where(valid, kin - (iota((256, 256), 1) >> 4) + 1, -9)


def head_matrices():
    row = iota((128, 16), 0)
    _, _, _, chan = packed((128, 16))
    second = (row >= 48) & (row < 96)
    rowrep = one_hot(second & (chan == iota((128, 16), 1)))
    row = iota((128, 256), 0)
    _, _, kin, _ = packed((128, 256))
    second = (row >= 48) & (row < 96)
    return rowrep, second & (kin == (iota((128, 256), 1) >> 4))


def shift_y(v, count, step):
    rows = v.shape[0]
    out = pltpu.roll(v, (-step) % rows, 0)
    if rows == count:
        return out
    if step == 1:
        other, edge = pltpu.roll(v, count - 1, 0), count - 1
    else:
        other, edge = pltpu.roll(v, rows - (count - 1), 0), 0
    spot = iota(v.shape, 0) & (count - 1)
    return jnp.where(spot == edge, other, out)


def silu_of(pre):
    half = 0.5 * pre
    return half + half * jnp.tanh(half)


def slope_of(pre):
    half = 0.5 * pre
    bend = jnp.tanh(half)
    return (0.5 + 0.5 * bend) * (1.0 + half * (1.0 - bend))


def prep_kernel(vel_ref, cot_ref, out_ref):
    row, col = iota((64, 128), 0), iota((64, 128), 1)
    mask = (row & 7) == (col >> 4)
    spread = one_hot((iota((64, 8), 0) >> 3) == iota((64, 8), 1))
    total = jnp.zeros((64, 128), F32)
    for part, ref in ((0, vel_ref), (1, cot_ref)):
        for chan in range(3):
            wide = mm(spread, ref[chan])
            kept = jnp.where(mask, wide, 0.0).astype(BF)
            place = one_hot(
                iota((128, 128), 1) - (part * 48 + chan) == 3 * (iota((128, 128), 0) & 15)
            )
            total = total + mm(kept, place)
    last = total[48:64]
    spare = iota((16, 128), 1) >= 96
    for g in range(3):
        moved = pltpu.roll(last, 96 - 32 * g, 1)
        rows = jnp.where(spare, moved, total[g * 16:(g + 1) * 16]).astype(BF)
        for copy in range(8):
            out_ref[copy, g * 16:(g + 1) * 16, :] = rows


def build_kernel(
    k1_far,
    k2_far,
    k3_far,
    k4_far,
    l4_far,
    l3_far,
    l2_far,
    head_far,
    t1,
    t2,
    t3,
    t4,
    f4,
    f3,
    f2,
    hp,
    b4,
    b3,
    b2,
    small,
    k1_ref,
    k2_ref,
    k3_ref,
    k4_ref,
    l4_ref,
    l3_ref,
    l2_ref,
    head_ref,
    sems,
):
    far = (k2_far, k3_far, k4_far, k1_far, l4_far, l3_far, l2_far, head_far)
    near = (k2_ref, k3_ref, k4_ref, k1_ref, l4_ref, l3_ref, l2_ref, head_ref)
    copies = [
        pltpu.make_async_copy(source, target, sems.at[i])
        for i, (source, target) in enumerate(zip(far, near))
    ]
    for copy in copies:
        copy.start()
    band = band_matrix()
    valid, b_row, _, chan = packed((256, 128))
    base = jnp.where(valid, iota((256, 128), 1) - 32 * chan - 3 * b_row, -99)
    rowrep, headmask = head_matrices()
    for copy in copies:
        copy.wait()

    def build(kernel_ref, t_ref, outs, ins):
        planes = 128 // ins
        rep = mm(kernel_ref[...], tile_matrix(outs, 256))
        kout = iota((ins, 256), 1) >> log2(outs)
        for ab in range(9):
            a, b = ab // 3, ab % 3
            taps = [rep[(ab * 3 + c) * ins:(ab * 3 + c + 1) * ins] for c in range(3)]
            for k in range(planes):
                block = jnp.zeros((ins, 256), F32)
                for c in range(3):
                    if 0 <= k - c + 1 < planes:
                        block = jnp.where(kout == k - c + 1, taps[c], block)
                start = b * 128 + k * ins
                t_ref[a, start:start + ins, :] = block.astype(BF)

    build(k2_ref, t2, 32, 16)
    build(k3_ref, t3, 64, 32)
    build(k4_ref, t4, 128, 64)
    small[...] = jnp.zeros(small.shape, F32)
    for c in range(3):
        small[c * 32:c * 32 + 27, :] = mm_tn(k1_ref[c], tile_matrix(16, 256))
    rep1 = small[...].astype(BF)
    for a in range(3):
        block = jnp.zeros((256, 256), F32)
        for c in range(3):
            block = jnp.where(band == c, mm(one_hot(base == 9 * a + c), rep1), block)
        t1[a] = block.astype(BF)

    def lift(lift_ref, f_ref, b_ref, coarse):
        fine, chans = lift_ref.shape
        rep = mm(lift_ref[...], tile_matrix(chans, 256))
        kin = iota((fine, 256), 1) >> log2(chans)
        for k in range(2 * coarse):
            f_ref[k * fine:(k + 1) * fine, :] = jnp.where(kin == k // 2, rep, 0.0).astype(BF)
        for k in range(coarse):
            b_ref[k * fine:(k + 1) * fine, :] = jnp.where(kin == k, rep, 0.0).astype(BF)

    lift(l4_ref, f4, b4, 2)
    lift(l3_ref, f3, b3, 4)
    lift(l2_ref, f2, b2, 8)
    small[0:16, 0:128] = jnp.zeros((16, 128), F32)
    small[0:3, 0:16] = head_ref[...].astype(F32)
    tileh = one_hot(iota((128, 256), 0) == (iota((128, 256), 1) & 15))
    reph = mm(small[0:16, 0:128].astype(BF), tileh).astype(BF)
    hp[...] = jnp.where(headmask, mm(rowrep, reph), 0.0).astype(BF)


def main_kernel(
    where_ref,
    own_far,
    tiles_far,
    t1_far,
    t2_far,
    t3_far,
    t4_far,
    f4_far,
    f3_far,
    f2_far,
    hp_far,
    b4_far,
    b3_far,
    b2_far,
    pred_ref,
    gradv_ref,
    share_ref,
    xt,
    xc,
    v3,
    pre1,
    act1,
    pre2,
    act2,
    pre3,
    act3,
    p32,
    p33,
    p34,
    skip1,
    carry2,
    carry3,
    back2,
    back3,
    d1,
    d2,
    d3,
    d4,
    ret2,
    tmp,
    ups_a,
    ups_b,
    line,
    pack,
    own_ref,
    tiles_ref,
    t1,
    t2,
    t3,
    t4,
    f4,
    f3,
    f2,
    hp,
    b4,
    b3,
    b2,
    sems,
):
    far = (t1_far, t2_far, t3_far, t4_far, f4_far, f3_far, f2_far, hp_far, b4_far, b3_far, b2_far)
    near = (t1, t2, t3, t4, f4, f3, f2, hp, b4, b3, b2)
    copies = [
        pltpu.make_async_copy(source, target, sems.at[9 + i])
        for i, (source, target) in enumerate(zip(far, near))
    ]
    own_copy = pltpu.make_async_copy(own_far, own_ref, sems.at[8])
    own_copy.start()

    def line_copy(step):
        return pltpu.make_async_copy(tiles_far.at[step], tiles_ref.at[step], sems.at[step])

    for step in range(8):
        line_copy(step).start()
    for copy in copies:
        copy.start()
    own_part = where_ref[0]
    lane = iota((1, 128), 1)
    band = band_matrix()
    valid, b_row, _, chan_row = packed((256, 16))
    pick = one_hot(valid & (iota((256, 16), 1) == 3 * b_row + chan_row))
    rowrep, headmask = head_matrices()

    pool1, pool2, pool3 = pool_matrix(16), pool_matrix(32), pool_matrix(64)

    def rows(start, count, unit):
        return pl.ds(pl.multiple_of(start, unit), count)

    v3[0:64, :] = jnp.zeros((64, 256), BF)
    v3[73 * 64:74 * 64, :] = jnp.zeros((64, 256), BF)

    def arrange(source, number):
        for n in range(8):
            tile = source(n).astype(F32)
            last = jnp.zeros((16, 128), F32)
            for g in range(3):
                moved = pltpu.roll(tile[g * 16:(g + 1) * 16], 32 * (g + 1), 1)
                last = jnp.where((lane >= 32 * g) & (lane < 32 * g + 32), moved, last)
            for i in range(8):
                piece = tile[i * 8:i * 8 + 8] if i < 6 else last[(i - 6) * 8:(i - 5) * 8]
                xt[i * 64 + n * 8:i * 64 + n * 8 + 8, :] = piece
        for i in range(8):
            row = xt[i * 64:(i + 1) * 64, :]
            xc[rows((number * 8 + i) * 64, 64, 64), :] = row.astype(BF)
            vel = jnp.where(lane < 48, row, 0.0)
            low = pltpu.roll(vel, 1, 0) + pltpu.roll(vel, 48, 1)
            high = pltpu.roll(vel, 63, 0)
            spot = rows((number * 8 + i + 1) * 64, 64, 64)
            v3[spot, 0:128] = low.astype(BF)
            v3[spot, 128:256] = high.astype(BF)

    def arrange_far(step, _):
        line_copy(step).wait()
        arrange(lambda n: tiles_ref[step, n], where_ref[1 + step])
        return 0

    own_copy.wait()
    arrange(lambda n: own_ref[n], 4)
    lax.fori_loop(0, 8, arrange_far, 0)
    for copy in copies:
        copy.wait()

    def pooled(field, matrix, count):
        flat = mm(field, matrix)
        pairs = field.shape[0] // (2 * count)
        for i in range(pairs):
            tmp[i * count:(i + 1) * count, :] = (
                flat[2 * i * count:(2 * i + 1) * count] + flat[(2 * i + 1) * count:(2 * i + 2) * count]
            )
        n = pairs * count // 2
        return tmp[pl.ds(0, n, stride=2), :] + tmp[pl.ds(1, n, stride=2), :]

    def enlarged(field, count):
        n = field.shape[0]
        for half, ref in ((0, ups_a), (1, ups_b)):
            piece = field[:, half * 128:(half + 1) * 128]
            ref[pl.ds(0, n, stride=2), :] = piece
            ref[pl.ds(1, n, stride=2), :] = piece
        big = jnp.concatenate([ups_a[0:2 * n, :], ups_b[0:2 * n, :]], axis=1)
        wide = 2 * count
        parts = []
        for i in range(n // count):
            piece = big[i * wide:(i + 1) * wide]
            parts += [piece, piece]
        return jnp.concatenate(parts, axis=0)

    def put3(ref, start, unit, field, count):
        spot = rows(start, field.shape[0], unit)
        kind = ref.dtype
        ref[spot, 0:128] = shift_y(field, count, -1).astype(kind)
        ref[spot, 128:256] = field.astype(kind)
        ref[spot, 256:384] = shift_y(field, count, 1).astype(kind)

    def fine_forward(step, _):
        start = step * 512
        pre = mm(v3[rows(start, 512, 64), :], t1[0])
        for a in (1, 2):
            pre = pre + mm(v3[rows(start + a * 64, 512, 64), :], t1[a])
        pre1[rows(start, 512, 512), :] = pre
        act = silu_of(pre).astype(BF)
        act1[rows(start, 512, 512), :] = act
        half = (pooled(act, pool1, 64) * 0.125).astype(BF).astype(F32)
        put3(p32, step * 128, 32, half, 32)
        return 0

    lax.fori_loop(0, 9, fine_forward, 0)

    def mid_forward(step, _):
        start = (2 + step * 8) * 32
        pre = mm(p32[rows(start - 32, 256, 32), :], t2[0])
        for a in (1, 2):
            pre = pre + mm(p32[rows(start + (a - 1) * 32, 256, 32), :], t2[a])
        pre2[rows(start, 256, 32), :] = pre
        act = silu_of(pre).astype(BF)
        act2[rows(start, 256, 32), :] = act
        half = (pooled(act, pool2, 32) * 0.125).astype(BF).astype(F32)
        put3(p33, (1 + step * 4) * 16, 16, half, 16)
        return 0

    lax.fori_loop(0, 4, mid_forward, 0)

    pre = mm(p33[16:240, :], t3[0])
    for a in (1, 2):
        pre = pre + mm(p33[(1 + a) * 16:(1 + a) * 16 + 224, :], t3[a])
    pre3[...] = pre
    act = silu_of(pre).astype(BF)
    act3[...] = act
    half = (pooled(act, pool3, 16) * 0.125).astype(BF).astype(F32)
    put3(p34, 8, 8, half, 8)

    pre4 = mm(p34[8:48, :].astype(BF), t4[0])
    for a in (1, 2):
        pre4 = pre4 + mm(p34[(1 + a) * 8:(1 + a) * 8 + 40, :].astype(BF), t4[a])
    act4 = silu_of(pre4)[16:24].astype(BF)

    skip3 = (act3[96:128, :].astype(F32) + enlarged(mm_nt(act4, f4[...]), 8)).astype(BF)
    skip2 = (act2[512:640, :].astype(F32) + enlarged(mm_nt(skip3, f3[...]), 16)).astype(BF)
    up2 = mm_nt(skip2, f2[...])
    for half in range(2):
        base = act1[2048 + half * 256:2304 + half * 256, :].astype(F32)
        up = enlarged(up2[half * 64:(half + 1) * 64], 32)
        skip1[half * 256:(half + 1) * 256, :] = (base + up).astype(BF)
    gh = mm_tn(xc[2048:2560, :], skip1[...])

    def fine_carry(step, _):
        back = mm(xc[rows((16 + step * 8) * 64, 512, 512), :], hp[...]).astype(BF)
        carry2[rows((8 + step * 4) * 32, 128, 128), :] = pooled(back, pool1, 64).astype(BF)
        return 0

    lax.fori_loop(0, 5, fine_carry, 0)

    for step in range(5):
        start = (8 + step * 4) * 32
        back = mm(carry2[start:start + 128, :], b2[...]).astype(BF)
        back2[start:start + 128, :] = back
        carry3[step * 32:(step + 1) * 32, :] = pooled(back, pool2, 32).astype(BF)
    back = mm(carry3[...], b3[...]).astype(BF)
    back3[...] = back
    carry4 = pooled(back, pool3, 16)

    gl2 = mm_tn(carry2[512:640, :], skip2)
    gl3 = mm_tn(carry3[64:96, :], skip3)
    gl4 = mm_tn(carry4[16:24].astype(BF), act4)

    delta4 = (mm(carry4.astype(BF), b4[...]) * slope_of(pre4)).astype(BF).astype(F32)
    d4[...] = delta4
    own4 = delta4[16:24].astype(BF)

    def returned(total, count):
        return (
            shift_y(total[:, 0:128], count, 1)
            + total[:, 128:256]
            + shift_y(total[:, 256:384], count, -1)
        )

    total = mm_nt(d4[16:40, :].astype(BF), t4[0])
    for a in (1, 2):
        total = total + mm_nt(d4[(2 - a) * 8:(2 - a) * 8 + 24, :].astype(BF), t4[a])
    ret4 = returned(total, 8)

    def spread_up(field, matrix, count):
        high, low = halves(field * 0.125)
        return enlarged(mm_nt(high, matrix) + mm_nt(low, matrix), count)

    slope = back3[32:128, :].astype(F32) + spread_up(ret4, pool3, 8)
    d3[...] = (slope * slope_of(pre3[64:160, :])).astype(BF)
    total = mm_nt(d3[32:96, :], t3[0])
    for a in (1, 2):
        total = total + mm_nt(d3[(2 - a) * 16:(2 - a) * 16 + 64, :], t3[a])
    ret3 = returned(total, 16)

    slope = back2[14 * 32:22 * 32, :].astype(F32) + spread_up(ret3, pool2, 16)
    d2[...] = (slope * slope_of(pre2[14 * 32:22 * 32, :])).astype(BF)
    total = mm_nt(d2[64:256, :], t2[0])
    for a in (1, 2):
        total = total + mm_nt(d2[(2 - a) * 32:(2 - a) * 32 + 192, :], t2[a])
    ret2[...] = returned(total, 32)

    for step in range(3):
        spot = slice((30 + step * 4) * 64, (34 + step * 4) * 64)
        up = spread_up(ret2[step * 64:(step + 1) * 64, :], pool1, 32)
        back = mm(xc[spot, :], hp[...]).astype(BF).astype(F32)
        d1[step * 256:(step + 1) * 256, :] = ((back + up) * slope_of(pre1[spot, :])).astype(BF)

    guess = mm_nt(skip1[...], hp[...])
    total = mm_nt(d1[192:704, :], t1[0])
    for a in (1, 2):
        total = total + mm_nt(d1[(3 - a) * 64:(3 - a) * 64 + 512, :], t1[a])
    low, high = total[:, 0:128], total[:, 128:256]
    grad = shift_y(low, 64, 1) + pltpu.roll(low, 80, 1) + shift_y(high, 64, -1)
    line[...] = jnp.where(lane < 48, grad, guess)
    pieces = [line[rows(i * 64 + own_part * 8, 8, 8), :] for i in range(8)]
    own = jnp.concatenate(pieces, axis=0)
    first, rest = halves(own)
    second, third = halves(own - first.astype(F32))
    mask = (iota((64, 128), 0) & 7) == (iota((64, 128), 1) >> 4)
    for part, ref in ((0, gradv_ref), (1, pred_ref)):
        for chan in range(3):
            matrix = one_hot(
                iota((128, 128), 0) - (part * 48 + chan) == 3 * (iota((128, 128), 1) & 15)
            )
            full = mm(first, matrix) + mm(second, matrix) + mm(third, matrix)
            full = jnp.where(mask, full, 0.0).reshape(8, 8, 128)
            ref[chan] = jnp.sum(full, axis=1)

    pack[1728:PACK, :] = jnp.zeros((PACK - 1728, 128), F32)

    def fold_taps(product, outs, ins, a, b):
        planes = 128 // ins
        kout = iota((ins, 256), 1) >> log2(outs)
        sums = [jnp.zeros((ins, 256), F32) for _ in range(3)]
        for k in range(planes):
            block = product[b * 128 + k * ins:b * 128 + (k + 1) * ins]
            for c in range(3):
                if 0 <= k - c + 1 < planes:
                    sums[c] = sums[c] + jnp.where(kout == k - c + 1, block, 0.0)
        joined = jnp.concatenate(sums, axis=0)
        joined = joined[:, 0:128] + joined[:, 128:256]
        width = outs
        while width < 128:
            joined = joined + pltpu.roll(joined, 128 - width, 1)
            width *= 2
        return joined

    fold4, fold2 = fold_matrix(256, 128, 0), fold_matrix(256, 32, 64)
    for a in range(3):
        product = mm_tn(p34[(3 + a) * 8:(4 + a) * 8, :].astype(BF), own4)
        for b in range(3):
            start = (a * 3 + b) * 192
            pack[start:start + 192, :] = fold_taps(product, 128, 64, a, b)
    for a in range(3):
        product = mm_tn(p33[(7 + a) * 16:(9 + a) * 16, :], d3[32:64, :])
        for b in range(3):
            part = fold_taps(product, 64, 32, a, b)
            left = jnp.where(lane < 64, part, 0.0)
            start = 1728 + (a * 3 + b) * 96
            if a * 3 + b < 8:
                pack[start:start + 96, :] = left
            else:
                pack[2496:2560, :] = left[0:64]
                pack[2352:2384, :] += jnp.where(lane >= 64, part[64:96], 0.0)
    for a in range(3):
        product = mm_tn(p32[(15 + a) * 32:(19 + a) * 32, :], d2[64:192, :])
        for b in range(3):
            part = fold_taps(product, 32, 16, a, b)
            start = 1728 + (a * 3 + b) * 48
            pack[start:start + 48, :] += jnp.where((lane >= 64) & (lane < 96), part, 0.0)
    fold1 = fold_matrix(256, 16, 96)
    for a in range(3):
        product = mm_tn(v3[(32 + a) * 64:(40 + a) * 64, :], d1[128:640, :])
        for c in range(3):
            high, low = halves(jnp.where(band == c, product, 0.0))
            sums = mm_tn(pick, high) + mm_tn(pick, low)
            start = 1728 + (a * 3 + c) * 16
            pack[start:start + 16, :] += mm2(sums, fold1)

    def fold_lift(product, fine, chans, matrix):
        kin = iota((fine, 256), 1) >> log2(chans)
        total = jnp.zeros((fine, 256), F32)
        for k in range(256 // chans):
            total = total + jnp.where(kin == k, product[k * fine:(k + 1) * fine], 0.0)
        return mm2(total, matrix)

    pack[2160:2192, :] += fold_lift(gl3, 32, 64, fold_matrix(256, 64, 64))
    pack[2192:2208, :] += fold_lift(gl2, 16, 32, fold2)
    high, low = halves(jnp.where(headmask, gh, 0.0))
    heads = mm_tn(rowrep, high) + mm_tn(rowrep, low)
    pack[2208:2224, :] += mm2(heads, fold_matrix(256, 16, 64))
    lift4 = fold_lift(gl4, 64, 128, fold4)
    pack[2224:2288, :] += jnp.where(lane >= 64, pltpu.roll(lift4, 64, 1), 0.0)
    pack[2288:2352, :] += jnp.where(lane >= 64, lift4, 0.0)
    share_ref[...] = pack[rows(own_part * SHARE, SHARE, SHARE), :].astype(BF)


def unpack_kernel(full_ref, order_ref, g1_ref, g2_ref, g3_ref, g4_ref, l4_ref, l3_ref, l2_ref, head_ref):
    scale = float(512 * 64 * 16) ** -0.5

    def left(start, count):
        return full_ref[start:start + count, :].astype(F32) * scale

    def right(start, count):
        return pltpu.roll(left(start, count), 64, 1)

    g4_ref[...] = left(0, 1728)
    g3_ref[0:832, :] = left(1728, 832)[:, 0:64]
    g3_ref[832:864, :] = right(2352, 32)[:, 0:64]
    g2_ref[...] = right(1728, 432)[:, 0:32]
    for c in range(3):
        turned = mm_tn(full_ref[1728:1872, :], order_ref[c]) * scale
        g1_ref[c] = turned[96:112, 0:27]
    l3_ref[...] = right(2160, 32)[:, 0:64]
    l2_ref[...] = right(2192, 16)[:, 0:32]
    head_ref[...] = right(2208, 16)[0:3, 0:16]
    l4_ref[:, 0:64] = right(2224, 64)[:, 0:64]
    l4_ref[:, 64:128] = left(2288, 64)[:, 64:128]


def order_matrix():
    order = np.zeros((3, 144, 128), np.float32)
    for tap in range(27):
        a, b, step = tap // 9, tap // 3 % 3, tap % 3
        for c in range(3):
            order[c, (a * 3 + step) * 16 + b * 3 + c, tap] = 1.0
    return order


def run_build(weights, interpret=False):
    k1, k2, k3, k4, l4, l3, l2, head = weights
    shapes = ((3, 256, 256),) + ((3, 384, 256),) * 3 + ((256, 256),) * 3 + ((128, 256),) * 4
    return pl.pallas_call(
        build_kernel,
        out_shape=tuple(jax.ShapeDtypeStruct(shape, BF) for shape in shapes),
        in_specs=[pl.BlockSpec(memory_space=pltpu.HBM)] * 8,
        scratch_shapes=[
            pltpu.VMEM((128, 256), F32),
            pltpu.VMEM((3, 16, 27), BF),
            pltpu.VMEM((432, 32), BF),
            pltpu.VMEM((864, 64), BF),
            pltpu.VMEM((1728, 128), BF),
            pltpu.VMEM((64, 128), BF),
            pltpu.VMEM((32, 64), BF),
            pltpu.VMEM((16, 32), BF),
            pltpu.VMEM((3, 16), BF),
            pltpu.SemaphoreType.DMA((8,)),
        ],
        compiler_params=pltpu.CompilerParams(vmem_limit_bytes=60 * 1024 * 1024),
        interpret=interpret,
    )(
        k1.transpose(2, 1, 0),
        k2.transpose(0, 2, 1).reshape(432, 32),
        k3.transpose(0, 2, 1).reshape(864, 64),
        k4.transpose(0, 2, 1).reshape(1728, 128),
        l4,
        l3,
        l2,
        head,
    )


def run_main(where, own, tiles, matrices, interpret=False):
    vm = pl.BlockSpec(memory_space=pltpu.VMEM)

    def buf(shape, kind=BF):
        return pltpu.VMEM(shape, kind)

    scratch = [
        buf((512, 128), F32),
        buf((72 * 64, 128)),
        buf((74 * 64, 256)),
        buf((72 * 64, 256), F32),
        buf((72 * 64, 256)),
        buf((36 * 32, 256), F32),
        buf((36 * 32, 256)),
        buf((224, 256), F32),
        buf((224, 256)),
        buf((36 * 32, 384)),
        buf((18 * 16, 384)),
        buf((9 * 8, 384), F32),
        buf((512, 256)),
        buf((36 * 32, 128)),
        buf((160, 128)),
        buf((36 * 32, 256)),
        buf((160, 256)),
        buf((768, 256)),
        buf((256, 256)),
        buf((96, 256)),
        buf((40, 256), F32),
        buf((192, 128), F32),
        buf((256, 128), F32),
        buf((128, 128), F32),
        buf((128, 128), F32),
        buf((512, 128), F32),
        buf((PACK, 128), F32),
        buf((8, 48, 128)),
        buf((8, 8, 48, 128)),
        buf((3, 256, 256)),
        buf((3, 384, 256)),
        buf((3, 384, 256)),
        buf((3, 384, 256)),
        buf((256, 256)),
        buf((256, 256)),
        buf((256, 256)),
        buf((128, 256)),
        buf((128, 256)),
        buf((128, 256)),
        buf((128, 256)),
        pltpu.SemaphoreType.DMA((20,)),
    ]
    return pl.pallas_call(
        main_kernel,
        out_shape=(
            jax.ShapeDtypeStruct((3, 8, 128), F32),
            jax.ShapeDtypeStruct((3, 8, 128), F32),
            jax.ShapeDtypeStruct((SHARE, 128), BF),
        ),
        in_specs=[pl.BlockSpec(memory_space=pltpu.SMEM)]
        + [pl.BlockSpec(memory_space=pltpu.HBM)] * 13,
        out_specs=(vm, vm, vm),
        scratch_shapes=scratch,
        compiler_params=pltpu.CompilerParams(vmem_limit_bytes=60 * 1024 * 1024),
        interpret=interpret,
    )(
        where,
        own,
        tiles,
        *matrices,
    )


def run_prep(velocity, cotangent, interpret=False):
    return pl.pallas_call(
        prep_kernel,
        out_shape=jax.ShapeDtypeStruct((8, 48, 128), BF),
        interpret=interpret,
    )(velocity, cotangent)


def unpack(full, interpret=False):
    order = order_matrix()
    shapes = ((3, 16, 27), (432, 32), (864, 64), (1728, 128), (64, 128), (32, 64), (16, 32), (3, 16))
    g1, g2, g3, g4, l4, l3, l2, head = pl.pallas_call(
        unpack_kernel,
        out_shape=tuple(jax.ShapeDtypeStruct(shape, F32) for shape in shapes),
        interpret=interpret,
    )(full, jnp.asarray(order, BF))
    return (
        g1.transpose(2, 1, 0),
        g2.reshape(27, 16, 32).transpose(0, 2, 1),
        g3.reshape(27, 32, 64).transpose(0, 2, 1),
        g4.reshape(27, 64, 128).transpose(0, 2, 1),
        l4,
        l3,
        l2,
        head,
    )


FAR = (4, -1, -4, 1, 3, -2, -3, 2)
GROUP_Y = [[8 * z + y for y in range(8)] for z in range(8)]
GROUP_Z = [[8 * z + y for z in range(8)] for y in range(8)]


def exchange(x, groups):
    return lax.all_to_all(x, "wide", 0, 0, axis_index_groups=groups, tiled=True)


def local(velocity, cotangent, *weights):
    where = jnp.stack([lax.axis_index("narrow")] + [4 + step for step in FAR]).astype(jnp.int32)
    copies = run_prep(velocity, cotangent)
    own = lax.all_to_all(copies, "narrow", 0, 0, tiled=True)
    routes = [((w + FAR[n]) % 64 * 8 + n, w * 8 + n) for w in range(64) for n in range(8)]
    far = lax.ppermute(own, ("wide", "narrow"), routes)
    tiles = lax.all_gather(far, "narrow", axis=0)
    prediction, grad_velocity, share = run_main(where, own, tiles, run_build(weights))
    pieces = exchange(share.reshape(8, PIECE, 128), GROUP_Y)
    partial = pieces.astype(F32).sum(axis=0).astype(BF)
    pieces = exchange(jnp.broadcast_to(partial, (8, PIECE, 128)), GROUP_Z)
    total = pieces.astype(F32).sum(axis=0).astype(BF)
    whole = exchange(jnp.broadcast_to(total, (8, PIECE, 128)), GROUP_Y).reshape(SHARE, 128)
    full = lax.all_gather(whole, "narrow", axis=0).reshape(PACK, 128)
    return (prediction, grad_velocity) + unpack(full)


def solution(mesh):
    split = P(None, "wide", "narrow")
    return jax.shard_map(
        local,
        mesh=mesh,
        in_specs=(split, split) + (P(),) * 8,
        out_specs=(split, split) + (P(),) * 8,
        check_vma=False,
    )
```

```python
import jax
import jax.numpy as jnp
from jax import lax
from jax.experimental import pallas as pl
from jax.experimental.pallas import tpu as pltpu
from jax.sharding import PartitionSpec as P

BF = jnp.bfloat16
F32 = jnp.float32
NZ = 16
LINES = 9
PIECE = 80
SHARE = 8 * PIECE
PACK = 4 * SHARE
PLACES = {
    "t1": (0, 256),
    "t2": (768, 384),
    "t3": (1920, 384),
    "t4": (3072, 384),
    "f4": (4224, 256),
    "f3": (4480, 256),
    "f2": (4736, 256),
    "hp": (4992, 128),
    "b4": (5120, 128),
    "b3": (5248, 128),
    "b2": (5376, 128),
}
WEIGHT_ROWS = 5504


def mm(a, b):
    return lax.dot_general(a, b, (((1,), (0,)), ((), ())), preferred_element_type=F32)


def mm_nt(a, b):
    return lax.dot_general(a, b, (((1,), (1,)), ((), ())), preferred_element_type=F32)


def mm_tn(a, b):
    return lax.dot_general(a, b, (((0,), (0,)), ((), ())), preferred_element_type=F32)


def halves(x):
    high = x.astype(BF)
    return high, (x - high.astype(F32)).astype(BF)


def taken(weights, name):
    start, count = PLACES[name]
    return weights[start:start + count, :]


def joint(parts, weights, name):
    start, count = PLACES[name]
    return mm(jnp.concatenate(parts, axis=1), weights[start:start + 3 * count, :])


def joint_nt(parts, weights, name):
    start, count = PLACES[name]
    matrix = [weights[start + a * count:start + (a + 1) * count, :] for a in range(3)]
    return mm_nt(jnp.concatenate(parts, axis=1), jnp.concatenate(matrix, axis=1))


def mm2(x, e):
    high, low = halves(x)
    return mm(high, e) + mm(low, e)


def iota(shape, axis):
    return lax.broadcasted_iota(jnp.int32, shape, axis)


def log2(n):
    return int(n).bit_length() - 1


def one_hot(mask):
    return jnp.where(mask, 1.0, 0.0).astype(BF)


def pool_matrix(chans):
    row, col = iota((256, 128), 0), iota((256, 128), 1)
    shift = log2(chans)
    same = (row & (chans - 1)) == (col & (chans - 1))
    return one_hot(same & ((row >> (shift + 1)) == (col >> shift)))


def tile_matrix(chans, lanes):
    return one_hot(iota((chans, lanes), 0) == (iota((chans, lanes), 1) & (chans - 1)))


def fold_matrix(rows, chans, lead):
    row, col = iota((rows, 128), 0), iota((rows, 128), 1)
    return one_hot((row & (chans - 1)) + lead == col)


def packed(shape):
    row = iota(shape, 0)
    b = jnp.where(row < 48, 0, jnp.where(row < 96, 1, 2))
    left = row - jnp.where(row < 48, 0, jnp.where(row < 96, 48, 128))
    kin = (left * 43) >> 7
    valid = (row < 96) | ((row >= 128) & (row < 176))
    return valid, b, kin, left - 3 * kin


def band_matrix():
    valid, _, kin, _ = packed((256, 256))
    return jnp.where(valid, kin - (iota((256, 256), 1) >> 4) + 1, -9)


def head_matrices():
    row = iota((128, 16), 0)
    _, _, _, chan = packed((128, 16))
    second = (row >= 48) & (row < 96)
    rowrep = one_hot(second & (chan == iota((128, 16), 1)))
    row = iota((128, 256), 0)
    _, _, kin, _ = packed((128, 256))
    second = (row >= 48) & (row < 96)
    return rowrep, second & (kin == (iota((128, 256), 1) >> 4))


def shift_y(v, count, step):
    rows = v.shape[0]
    out = pltpu.roll(v, (-step) % rows, 0)
    if rows == count:
        return out
    if step == 1:
        other, edge = pltpu.roll(v, count - 1, 0), count - 1
    else:
        other, edge = pltpu.roll(v, rows - (count - 1), 0), 0
    spot = iota(v.shape, 0) & (count - 1)
    return jnp.where(spot == edge, other, out)


def silu_of(pre):
    half = 0.5 * pre
    return half + half * jnp.tanh(half)


def slope_of(pre):
    half = 0.5 * pre
    bend = jnp.tanh(half)
    return (0.5 + 0.5 * bend) * (1.0 + half * (1.0 - bend))


def prep_kernel(vel_ref, cot_ref, out_ref):
    row, col = iota((64, 128), 0), iota((64, 128), 1)
    mask = (row & 7) == (col >> 4)
    spread = one_hot((iota((64, 8), 0) >> 3) == iota((64, 8), 1))
    total = jnp.zeros((64, 128), F32)
    for part, ref in ((0, vel_ref), (1, cot_ref)):
        for chan in range(3):
            wide = mm(spread, ref[chan])
            kept = jnp.where(mask, wide, 0.0).astype(BF)
            place = one_hot(
                iota((128, 128), 1) - (part * 48 + chan) == 3 * (iota((128, 128), 0) & 15)
            )
            total = total + mm(kept, place)
    last = total[48:64]
    spare = iota((16, 128), 1) >= 96
    for g in range(3):
        moved = pltpu.roll(last, 96 - 32 * g, 1)
        rows = jnp.where(spare, moved, total[g * 16:(g + 1) * 16]).astype(BF)
        for copy in range(8):
            out_ref[copy, g * 16:(g + 1) * 16, :] = rows


def build_kernel(
    k1_far,
    k2_far,
    k3_far,
    k4_far,
    l4_far,
    l3_far,
    l2_far,
    head_far,
    weights,
    small,
    k1_ref,
    k2_ref,
    k3_ref,
    k4_ref,
    l4_ref,
    l3_ref,
    l2_ref,
    head_ref,
    sems,
):
    far = (k2_far, k3_far, k4_far, k1_far, l4_far, l3_far, l2_far, head_far)
    near = (k2_ref, k3_ref, k4_ref, k1_ref, l4_ref, l3_ref, l2_ref, head_ref)
    copies = [
        pltpu.make_async_copy(source, target, sems.at[i])
        for i, (source, target) in enumerate(zip(far, near))
    ]
    for copy in copies:
        copy.start()
    band = band_matrix()
    valid, b_row, _, chan = packed((256, 128))
    base = jnp.where(valid, iota((256, 128), 1) - 32 * chan - 3 * b_row, -99)
    rowrep, headmask = head_matrices()
    for copy in copies:
        copy.wait()

    def build(kernel_ref, place, outs, ins):
        planes = 128 // ins
        rep = mm(kernel_ref[...], tile_matrix(outs, 256))
        kout = iota((ins, 256), 1) >> log2(outs)
        for ab in range(9):
            a, b = ab // 3, ab % 3
            taps = [rep[(ab * 3 + c) * ins:(ab * 3 + c + 1) * ins] for c in range(3)]
            for k in range(planes):
                block = jnp.zeros((ins, 256), F32)
                for c in range(3):
                    if 0 <= k - c + 1 < planes:
                        block = jnp.where(kout == k - c + 1, taps[c], block)
                start = place + a * 384 + b * 128 + k * ins
                weights[start:start + ins, :] = block.astype(BF)

    build(k2_ref, PLACES["t2"][0], 32, 16)
    build(k3_ref, PLACES["t3"][0], 64, 32)
    build(k4_ref, PLACES["t4"][0], 128, 64)
    small[...] = jnp.zeros(small.shape, F32)
    for c in range(3):
        small[c * 32:c * 32 + 27, :] = mm_tn(k1_ref[c], tile_matrix(16, 256))
    rep1 = small[...].astype(BF)
    for a in range(3):
        block = jnp.zeros((256, 256), F32)
        for c in range(3):
            block = jnp.where(band == c, mm(one_hot(base == 9 * a + c), rep1), block)
        weights[a * 256:(a + 1) * 256, :] = block.astype(BF)

    def lift(lift_ref, up, back, coarse):
        fine, chans = lift_ref.shape
        rep = mm(lift_ref[...], tile_matrix(chans, 256))
        kin = iota((fine, 256), 1) >> log2(chans)
        for k in range(2 * coarse):
            start = PLACES[up][0] + k * fine
            weights[start:start + fine, :] = jnp.where(kin == k // 2, rep, 0.0).astype(BF)
        for k in range(coarse):
            start = PLACES[back][0] + k * fine
            weights[start:start + fine, :] = jnp.where(kin == k, rep, 0.0).astype(BF)

    lift(l4_ref, "f4", "b4", 2)
    lift(l3_ref, "f3", "b3", 4)
    lift(l2_ref, "f2", "b2", 8)
    small[0:16, 0:128] = jnp.zeros((16, 128), F32)
    small[0:3, 0:16] = head_ref[...].astype(F32)
    tileh = one_hot(iota((128, 256), 0) == (iota((128, 256), 1) & 15))
    reph = mm(small[0:16, 0:128].astype(BF), tileh).astype(BF)
    weights[4992:5120, :] = jnp.where(headmask, mm(rowrep, reph), 0.0).astype(BF)


def main_kernel(
    where_ref,
    own_ref,
    tiles_ref,
    twins_ref,
    weights_far,
    pred_ref,
    gradv_ref,
    share_ref,
    xt,
    xc,
    v3,
    pre1,
    act1,
    pre2,
    act2,
    pre3,
    act3,
    p32,
    p33,
    p34,
    skip1,
    carry2,
    carry3,
    back2,
    back3,
    d1,
    d2,
    d3,
    d4,
    ret2,
    tmp,
    ups_a,
    ups_b,
    line,
    pack,
    weights,
    sem,
):
    weights_copy = pltpu.make_async_copy(weights_far, weights, sem)
    weights_copy.start()
    own_part = where_ref[0]
    lane = iota((1, 128), 1)
    band = band_matrix()
    valid, b_row, _, chan_row = packed((256, 16))
    pick = one_hot(valid & (iota((256, 16), 1) == 3 * b_row + chan_row))
    rowrep, headmask = head_matrices()

    pool1, pool2, pool3 = pool_matrix(16), pool_matrix(32), pool_matrix(64)

    def rows(start, count, unit):
        return pl.ds(pl.multiple_of(start, unit), count)

    v3[0:64, :] = jnp.zeros((64, 256), BF)
    v3[73 * 64:74 * 64, :] = jnp.zeros((64, 256), BF)

    def arrange(source, number):
        for n in range(8):
            tile = source(n).astype(F32)
            last = jnp.zeros((16, 128), F32)
            for g in range(3):
                moved = pltpu.roll(tile[g * 16:(g + 1) * 16], 32 * (g + 1), 1)
                last = jnp.where((lane >= 32 * g) & (lane < 32 * g + 32), moved, last)
            for i in range(8):
                piece = tile[i * 8:i * 8 + 8] if i < 6 else last[(i - 6) * 8:(i - 5) * 8]
                xt[i * 64 + n * 8:i * 64 + n * 8 + 8, :] = piece
        for i in range(8):
            row = xt[i * 64:(i + 1) * 64, :]
            xc[rows((number * 8 + i) * 64, 64, 64), :] = row.astype(BF)
            vel = jnp.where(lane < 48, row, 0.0)
            low = pltpu.roll(vel, 1, 0) + pltpu.roll(vel, 48, 1)
            high = pltpu.roll(vel, 63, 0)
            spot = rows((number * 8 + i + 1) * 64, 64, 64)
            v3[spot, 0:128] = low.astype(BF)
            v3[spot, 128:256] = high.astype(BF)

    def arrange_tiles(step, _):
        arrange(lambda n: tiles_ref[step, n], where_ref[1 + step])
        return 0

    def arrange_twins(step, _):
        arrange(lambda n: twins_ref[step, n], where_ref[5 + step])
        return 0

    arrange(lambda n: own_ref[n], 4)
    lax.fori_loop(0, 4, arrange_tiles, 0)
    lax.fori_loop(0, 4, arrange_twins, 0)
    weights_copy.wait()

    def pooled(field, matrix, count):
        flat = mm(field, matrix)
        pairs = field.shape[0] // (2 * count)
        for i in range(pairs):
            tmp[i * count:(i + 1) * count, :] = (
                flat[2 * i * count:(2 * i + 1) * count] + flat[(2 * i + 1) * count:(2 * i + 2) * count]
            )
        n = pairs * count // 2
        return tmp[pl.ds(0, n, stride=2), :] + tmp[pl.ds(1, n, stride=2), :]

    def enlarged(field, count):
        n = field.shape[0]
        for half, ref in ((0, ups_a), (1, ups_b)):
            piece = field[:, half * 128:(half + 1) * 128]
            ref[pl.ds(0, n, stride=2), :] = piece
            ref[pl.ds(1, n, stride=2), :] = piece
        big = jnp.concatenate([ups_a[0:2 * n, :], ups_b[0:2 * n, :]], axis=1)
        wide = 2 * count
        parts = []
        for i in range(n // count):
            piece = big[i * wide:(i + 1) * wide]
            parts += [piece, piece]
        return jnp.concatenate(parts, axis=0)

    def put3(ref, start, unit, field, count):
        spot = rows(start, field.shape[0], unit)
        kind = ref.dtype
        ref[spot, 0:128] = shift_y(field, count, -1).astype(kind)
        ref[spot, 128:256] = field.astype(kind)
        ref[spot, 256:384] = shift_y(field, count, 1).astype(kind)

    def fine_forward(step, _):
        start = step * 512
        pre = joint([v3[rows(start + a * 64, 512, 64), :] for a in range(3)], weights, "t1")
        pre1[rows(start, 512, 512), :] = pre
        act = silu_of(pre).astype(BF)
        act1[rows(start, 512, 512), :] = act
        half = (pooled(act, pool1, 64) * 0.125).astype(BF).astype(F32)
        put3(p32, step * 128, 32, half, 32)
        return 0

    lax.fori_loop(0, 9, fine_forward, 0)

    def mid_forward(step, _):
        start = (2 + step * 8) * 32
        pre = joint([p32[rows(start + (a - 1) * 32, 256, 32), :] for a in range(3)], weights, "t2")
        pre2[rows(start, 256, 32), :] = pre
        act = silu_of(pre).astype(BF)
        act2[rows(start, 256, 32), :] = act
        half = (pooled(act, pool2, 32) * 0.125).astype(BF).astype(F32)
        put3(p33, (1 + step * 4) * 16, 16, half, 16)
        return 0

    lax.fori_loop(0, 4, mid_forward, 0)

    pre = joint([p33[(1 + a) * 16:(1 + a) * 16 + 224, :] for a in range(3)], weights, "t3")
    pre3[...] = pre
    act = silu_of(pre).astype(BF)
    act3[...] = act
    half = (pooled(act, pool3, 16) * 0.125).astype(BF).astype(F32)
    put3(p34, 8, 8, half, 8)

    pre4 = joint([p34[(1 + a) * 8:(1 + a) * 8 + 40, :].astype(BF) for a in range(3)], weights, "t4")
    act4 = silu_of(pre4)[16:24].astype(BF)

    skip3 = (act3[96:128, :].astype(F32) + enlarged(mm_nt(act4, taken(weights, "f4")), 8)).astype(BF)
    skip2 = (act2[512:640, :].astype(F32) + enlarged(mm_nt(skip3, taken(weights, "f3")), 16)).astype(BF)
    up2 = mm_nt(skip2, taken(weights, "f2"))
    for half in range(2):
        base = act1[2048 + half * 256:2304 + half * 256, :].astype(F32)
        up = enlarged(up2[half * 64:(half + 1) * 64], 32)
        skip1[half * 256:(half + 1) * 256, :] = (base + up).astype(BF)
    gh = mm_tn(xc[2048:2560, :], skip1[...])

    def fine_carry(step, _):
        back = mm(xc[rows((16 + step * 8) * 64, 512, 512), :], taken(weights, "hp")).astype(BF)
        carry2[rows((8 + step * 4) * 32, 128, 128), :] = pooled(back, pool1, 64).astype(BF)
        return 0

    lax.fori_loop(0, 5, fine_carry, 0)

    for step in range(5):
        start = (8 + step * 4) * 32
        back = mm(carry2[start:start + 128, :], taken(weights, "b2")).astype(BF)
        back2[start:start + 128, :] = back
        carry3[step * 32:(step + 1) * 32, :] = pooled(back, pool2, 32).astype(BF)
    back = mm(carry3[...], taken(weights, "b3")).astype(BF)
    back3[...] = back
    carry4 = pooled(back, pool3, 16)

    gl2 = mm_tn(carry2[512:640, :], skip2)
    gl3 = mm_tn(carry3[64:96, :], skip3)
    gl4 = mm_tn(carry4[16:24].astype(BF), act4)

    delta4 = (mm(carry4.astype(BF), taken(weights, "b4")) * slope_of(pre4)).astype(BF).astype(F32)
    d4[...] = delta4
    own4 = delta4[16:24].astype(BF)

    def returned(total, count):
        return (
            shift_y(total[:, 0:128], count, 1)
            + total[:, 128:256]
            + shift_y(total[:, 256:384], count, -1)
        )

    total = joint_nt([d4[(2 - a) * 8:(2 - a) * 8 + 24, :].astype(BF) for a in range(3)], weights, "t4")
    ret4 = returned(total, 8)

    def spread_up(field, matrix, count):
        high, low = halves(field * 0.125)
        return enlarged(mm_nt(high, matrix) + mm_nt(low, matrix), count)

    slope = back3[32:128, :].astype(F32) + spread_up(ret4, pool3, 8)
    d3[...] = (slope * slope_of(pre3[64:160, :])).astype(BF)
    total = joint_nt([d3[(2 - a) * 16:(2 - a) * 16 + 64, :] for a in range(3)], weights, "t3")
    ret3 = returned(total, 16)

    slope = back2[14 * 32:22 * 32, :].astype(F32) + spread_up(ret3, pool2, 16)
    d2[...] = (slope * slope_of(pre2[14 * 32:22 * 32, :])).astype(BF)
    total = joint_nt([d2[(2 - a) * 32:(2 - a) * 32 + 192, :] for a in range(3)], weights, "t2")
    ret2[...] = returned(total, 32)

    for step in range(3):
        spot = slice((30 + step * 4) * 64, (34 + step * 4) * 64)
        up = spread_up(ret2[step * 64:(step + 1) * 64, :], pool1, 32)
        back = mm(xc[spot, :], taken(weights, "hp")).astype(BF).astype(F32)
        d1[step * 256:(step + 1) * 256, :] = ((back + up) * slope_of(pre1[spot, :])).astype(BF)

    guess = mm_nt(skip1[...], taken(weights, "hp"))
    total = joint_nt([d1[(3 - a) * 64:(3 - a) * 64 + 512, :] for a in range(3)], weights, "t1")
    low, high = total[:, 0:128], total[:, 128:256]
    grad = shift_y(low, 64, 1) + pltpu.roll(low, 80, 1) + shift_y(high, 64, -1)
    line[...] = jnp.where(lane < 48, grad, guess)
    pieces = [line[rows(i * 64 + own_part * 8, 8, 8), :] for i in range(8)]
    own = jnp.concatenate(pieces, axis=0)
    first, rest = halves(own)
    second, third = halves(own - first.astype(F32))
    mask = (iota((64, 128), 0) & 7) == (iota((64, 128), 1) >> 4)
    for part, ref in ((0, gradv_ref), (1, pred_ref)):
        for chan in range(3):
            matrix = one_hot(
                iota((128, 128), 0) - (part * 48 + chan) == 3 * (iota((128, 128), 1) & 15)
            )
            full = mm(first, matrix) + mm(second, matrix) + mm(third, matrix)
            full = jnp.where(mask, full, 0.0).reshape(8, 8, 128)
            ref[chan] = jnp.sum(full, axis=1)

    pack[1728:PACK, :] = jnp.zeros((PACK - 1728, 128), F32)

    def fold_taps(product, outs, ins, a, b):
        planes = 128 // ins
        kout = iota((ins, 256), 1) >> log2(outs)
        sums = [jnp.zeros((ins, 256), F32) for _ in range(3)]
        for k in range(planes):
            block = product[b * 128 + k * ins:b * 128 + (k + 1) * ins]
            for c in range(3):
                if 0 <= k - c + 1 < planes:
                    sums[c] = sums[c] + jnp.where(kout == k - c + 1, block, 0.0)
        joined = jnp.concatenate(sums, axis=0)
        joined = joined[:, 0:128] + joined[:, 128:256]
        width = outs
        while width < 128:
            joined = joined + pltpu.roll(joined, 128 - width, 1)
            width *= 2
        return joined

    fold4, fold2 = fold_matrix(256, 128, 0), fold_matrix(256, 32, 64)
    for a in range(3):
        product = mm_tn(p34[(3 + a) * 8:(4 + a) * 8, :].astype(BF), own4)
        for b in range(3):
            start = (a * 3 + b) * 192
            pack[start:start + 192, :] = fold_taps(product, 128, 64, a, b)
    for a in range(3):
        product = mm_tn(p33[(7 + a) * 16:(9 + a) * 16, :], d3[32:64, :])
        for b in range(3):
            part = fold_taps(product, 64, 32, a, b)
            left = jnp.where(lane < 64, part, 0.0)
            start = 1728 + (a * 3 + b) * 96
            if a * 3 + b < 8:
                pack[start:start + 96, :] = left
            else:
                pack[2496:2560, :] = left[0:64]
                pack[2352:2384, :] += jnp.where(lane >= 64, part[64:96], 0.0)
    for a in range(3):
        product = mm_tn(p32[(15 + a) * 32:(19 + a) * 32, :], d2[64:192, :])
        for b in range(3):
            part = fold_taps(product, 32, 16, a, b)
            start = 1728 + (a * 3 + b) * 48
            pack[start:start + 48, :] += jnp.where((lane >= 64) & (lane < 96), part, 0.0)
    fold1 = fold_matrix(256, 16, 96)
    for a in range(3):
        product = mm_tn(v3[(32 + a) * 64:(40 + a) * 64, :], d1[128:640, :])
        for c in range(3):
            high, low = halves(jnp.where(band == c, product, 0.0))
            sums = mm_tn(pick, high) + mm_tn(pick, low)
            start = 1728 + (a * 3 + c) * 16
            pack[start:start + 16, :] += mm2(sums, fold1)

    def fold_lift(product, fine, chans, matrix):
        kin = iota((fine, 256), 1) >> log2(chans)
        total = jnp.zeros((fine, 256), F32)
        for k in range(256 // chans):
            total = total + jnp.where(kin == k, product[k * fine:(k + 1) * fine], 0.0)
        return mm2(total, matrix)

    pack[2160:2192, :] += fold_lift(gl3, 32, 64, fold_matrix(256, 64, 64))
    pack[2192:2208, :] += fold_lift(gl2, 16, 32, fold2)
    high, low = halves(jnp.where(headmask, gh, 0.0))
    heads = mm_tn(rowrep, high) + mm_tn(rowrep, low)
    pack[2208:2224, :] += mm2(heads, fold_matrix(256, 16, 64))
    lift4 = fold_lift(gl4, 64, 128, fold4)
    pack[2224:2288, :] += jnp.where(lane >= 64, pltpu.roll(lift4, 64, 1), 0.0)
    pack[2288:2352, :] += jnp.where(lane >= 64, lift4, 0.0)
    share_ref[...] = pack[rows(where_ref[9] * SHARE, SHARE, SHARE), :].astype(BF)


def unpack_kernel(
    full_ref, g1_ref, g2_ref, g3_ref, g4_ref, l4_ref, l3_ref, l2_ref, head_ref
):
    scale = float(512 * 64 * 16) ** -0.5
    row, col = iota((144, 128), 0), iota((144, 128), 1)
    a_step, spot = row >> 4, row & 15
    b_row, a_row = (spot * 11) >> 5, (a_step * 11) >> 5
    tap = 9 * a_row + 3 * b_row + a_step - 3 * a_row
    chan = jnp.where(spot < 9, spot - 3 * b_row, -1)

    def left(start, count):
        return full_ref[start:start + count, :].astype(F32) * scale

    def right(start, count):
        return pltpu.roll(left(start, count), 64, 1)

    g4_ref[...] = left(0, 1728)
    g3_ref[0:832, :] = left(1728, 832)[:, 0:64]
    g3_ref[832:864, :] = right(2352, 32)[:, 0:64]
    g2_ref[...] = right(1728, 432)[:, 0:32]
    for c in range(3):
        turned = mm_tn(full_ref[1728:1872, :], one_hot((chan == c) & (col == tap))) * scale
        g1_ref[c] = turned[96:112, 0:27]
    l3_ref[...] = right(2160, 32)[:, 0:64]
    l2_ref[...] = right(2192, 16)[:, 0:32]
    head_ref[...] = right(2208, 16)[0:3, 0:16]
    l4_ref[:, 0:64] = right(2224, 64)[:, 0:64]
    l4_ref[:, 64:128] = left(2288, 64)[:, 64:128]


def run_build(weights, interpret=False):
    k1, k2, k3, k4, l4, l3, l2, head = weights
    return pl.pallas_call(
        build_kernel,
        out_shape=jax.ShapeDtypeStruct((WEIGHT_ROWS, 256), BF),
        in_specs=[pl.BlockSpec(memory_space=pltpu.HBM)] * 8,
        scratch_shapes=[
            pltpu.VMEM((128, 256), F32),
            pltpu.VMEM((3, 16, 27), BF),
            pltpu.VMEM((432, 32), BF),
            pltpu.VMEM((864, 64), BF),
            pltpu.VMEM((1728, 128), BF),
            pltpu.VMEM((64, 128), BF),
            pltpu.VMEM((32, 64), BF),
            pltpu.VMEM((16, 32), BF),
            pltpu.VMEM((3, 16), BF),
            pltpu.SemaphoreType.DMA((8,)),
        ],
        compiler_params=pltpu.CompilerParams(vmem_limit_bytes=60 * 1024 * 1024),
        interpret=interpret,
    )(
        k1.transpose(2, 1, 0),
        k2.transpose(0, 2, 1).reshape(432, 32),
        k3.transpose(0, 2, 1).reshape(864, 64),
        k4.transpose(0, 2, 1).reshape(1728, 128),
        l4,
        l3,
        l2,
        head,
    )


def run_main(where, own, tiles, twins, matrix, interpret=False):
    vm = pl.BlockSpec(memory_space=pltpu.VMEM)

    def buf(shape, kind=BF):
        return pltpu.VMEM(shape, kind)

    scratch = [
        buf((512, 128), F32),
        buf((72 * 64, 128)),
        buf((74 * 64, 256)),
        buf((72 * 64, 256), F32),
        buf((72 * 64, 256)),
        buf((36 * 32, 256), F32),
        buf((36 * 32, 256)),
        buf((224, 256), F32),
        buf((224, 256)),
        buf((36 * 32, 384)),
        buf((18 * 16, 384)),
        buf((9 * 8, 384), F32),
        buf((512, 256)),
        buf((36 * 32, 128)),
        buf((160, 128)),
        buf((36 * 32, 256)),
        buf((160, 256)),
        buf((768, 256)),
        buf((256, 256)),
        buf((96, 256)),
        buf((40, 256), F32),
        buf((192, 128), F32),
        buf((256, 128), F32),
        buf((128, 128), F32),
        buf((128, 128), F32),
        buf((512, 128), F32),
        buf((PACK, 128), F32),
        buf((WEIGHT_ROWS, 256)),
        pltpu.SemaphoreType.DMA,
    ]
    return pl.pallas_call(
        main_kernel,
        out_shape=(
            jax.ShapeDtypeStruct((3, 8, 128), F32),
            jax.ShapeDtypeStruct((3, 8, 128), F32),
            jax.ShapeDtypeStruct((SHARE, 128), BF),
        ),
        in_specs=[pl.BlockSpec(memory_space=pltpu.SMEM)] + [vm] * 3 + [pl.BlockSpec(memory_space=pltpu.HBM)],
        out_specs=(vm, vm, vm),
        scratch_shapes=scratch,
        compiler_params=pltpu.CompilerParams(vmem_limit_bytes=52 * 1024 * 1024),
        interpret=interpret,
    )(
        where,
        own,
        tiles,
        twins,
        matrix,
    )


def run_prep(velocity, cotangent, interpret=False):
    return pl.pallas_call(
        prep_kernel,
        out_shape=jax.ShapeDtypeStruct((8, 48, 128), BF),
        interpret=interpret,
    )(velocity, cotangent)


def unpack(full, interpret=False):
    shapes = ((3, 16, 27), (432, 32), (864, 64), (1728, 128), (64, 128), (32, 64), (16, 32), (3, 16))
    g1, g2, g3, g4, l4, l3, l2, head = pl.pallas_call(
        unpack_kernel,
        out_shape=tuple(jax.ShapeDtypeStruct(shape, F32) for shape in shapes),
        interpret=interpret,
    )(full)
    return (
        g1.transpose(2, 1, 0),
        g2.reshape(27, 16, 32).transpose(0, 2, 1),
        g3.reshape(27, 32, 64).transpose(0, 2, 1),
        g4.reshape(27, 64, 128).transpose(0, 2, 1),
        l4,
        l3,
        l2,
        head,
    )


FAR = (4, -1, -4, 1, 3, -2, -3, 2)
GROUP_Y = [[8 * z + y for y in range(8)] for z in range(8)]
GROUP_Z = [[8 * z + y for z in range(8)] for y in range(8)]


def shared(x):
    copies = jnp.broadcast_to(x, (4,) + x.shape)
    groups = [[0, 2, 4, 6], [1, 3, 5, 7]]
    return lax.all_to_all(copies, "narrow", 0, 0, axis_index_groups=groups, tiled=True)


def exchange(x, groups):
    return lax.all_to_all(x, "wide", 0, 0, axis_index_groups=groups, tiled=True)


def local(velocity, cotangent, *weights):
    part = lax.axis_index("narrow")
    even, odd = ([4 + step for step in FAR[core::2]] for core in range(2))
    order = [jnp.where(part % 2 == 0, a, b) for a, b in zip(even + odd, odd + even)]
    where = jnp.stack([part] + order + [part // 2]).astype(jnp.int32)
    copies = run_prep(velocity, cotangent)
    own = lax.all_to_all(copies, "narrow", 0, 0, tiled=True)
    routes = [((w + FAR[n]) % 64 * 8 + n, w * 8 + n) for w in range(64) for n in range(8)]
    far = lax.ppermute(own, ("wide", "narrow"), routes)
    far, matrix = lax.optimization_barrier((far, run_build(weights)))
    tiles = shared(far)
    twins = lax.ppermute(tiles, "narrow", [(n, n ^ 1) for n in range(8)])
    prediction, grad_velocity, share = run_main(where, own, tiles, twins, matrix)
    pieces = exchange(share.reshape(8, PIECE, 128), GROUP_Y)
    partial = pieces.astype(F32).sum(axis=0).astype(BF)
    pieces = exchange(jnp.broadcast_to(partial, (8, PIECE, 128)), GROUP_Z)
    total = pieces.astype(F32).sum(axis=0).astype(BF)
    whole = exchange(jnp.broadcast_to(total, (8, PIECE, 128)), GROUP_Y).reshape(SHARE, 128)
    return (prediction, grad_velocity) + unpack(shared(whole).reshape(PACK, 128))


def solution(mesh):
    split = P(None, "wide", "narrow")
    return jax.shard_map(
        local,
        mesh=mesh,
        in_specs=(split, split) + (P(),) * 8,
        out_specs=(split, split) + (P(),) * 8,
        check_vma=False,
    )
```

```python
import jax
import jax.numpy as jnp
from jax import lax
from jax.experimental import pallas as pl
from jax.experimental.pallas import tpu as pltpu
from jax.sharding import PartitionSpec as P

BF = jnp.bfloat16
F32 = jnp.float32
NZ = 16
LINES = 9
PIECE = 80
SHARE = 8 * PIECE
PACK = 4 * SHARE
PLACES = {
    "t1": (0, 256),
    "t2": (768, 384),
    "t3": (1920, 384),
    "t4": (3072, 384),
    "f4": (4224, 256),
    "f3": (4480, 256),
    "f2": (4736, 256),
    "hp": (4992, 128),
    "b4": (5120, 128),
    "b3": (5248, 128),
    "b2": (5376, 128),
}
WEIGHT_ROWS = 5504


def mm(a, b):
    return lax.dot_general(a, b, (((1,), (0,)), ((), ())), preferred_element_type=F32)


def mm_nt(a, b):
    return lax.dot_general(a, b, (((1,), (1,)), ((), ())), preferred_element_type=F32)


def mm_tn(a, b):
    return lax.dot_general(a, b, (((0,), (0,)), ((), ())), preferred_element_type=F32)


def halves(x):
    high = x.astype(BF)
    return high, (x - high.astype(F32)).astype(BF)


def taken(weights, name):
    start, count = PLACES[name]
    return weights[start:start + count, :]


def joint(parts, weights, name):
    start, count = PLACES[name]
    return mm(jnp.concatenate(parts, axis=1), weights[start:start + 3 * count, :])


def joint_nt(parts, weights, name):
    start, count = PLACES[name]
    matrix = [weights[start + a * count:start + (a + 1) * count, :] for a in range(3)]
    return mm_nt(jnp.concatenate(parts, axis=1), jnp.concatenate(matrix, axis=1))


def mm2(x, e):
    high, low = halves(x)
    return mm(high, e) + mm(low, e)


def iota(shape, axis):
    return lax.broadcasted_iota(jnp.int32, shape, axis)


def log2(n):
    return int(n).bit_length() - 1


def one_hot(mask):
    return jnp.where(mask, 1.0, 0.0).astype(BF)


def pool_matrix(chans):
    row, col = iota((256, 128), 0), iota((256, 128), 1)
    shift = log2(chans)
    same = (row & (chans - 1)) == (col & (chans - 1))
    return one_hot(same & ((row >> (shift + 1)) == (col >> shift)))


def tile_matrix(chans, lanes):
    return one_hot(iota((chans, lanes), 0) == (iota((chans, lanes), 1) & (chans - 1)))


def fold_matrix(rows, chans, lead):
    row, col = iota((rows, 128), 0), iota((rows, 128), 1)
    return one_hot((row & (chans - 1)) + lead == col)


def packed(shape):
    row = iota(shape, 0)
    b = jnp.where(row < 48, 0, jnp.where(row < 96, 1, 2))
    left = row - jnp.where(row < 48, 0, jnp.where(row < 96, 48, 128))
    kin = (left * 43) >> 7
    valid = (row < 96) | ((row >= 128) & (row < 176))
    return valid, b, kin, left - 3 * kin


def band_matrix():
    valid, _, kin, _ = packed((256, 256))
    return jnp.where(valid, kin - (iota((256, 256), 1) >> 4) + 1, -9)


def head_matrices():
    row = iota((128, 16), 0)
    _, _, _, chan = packed((128, 16))
    second = (row >= 48) & (row < 96)
    rowrep = one_hot(second & (chan == iota((128, 16), 1)))
    row = iota((128, 256), 0)
    _, _, kin, _ = packed((128, 256))
    second = (row >= 48) & (row < 96)
    return rowrep, second & (kin == (iota((128, 256), 1) >> 4))


def shift_y(v, count, step):
    rows = v.shape[0]
    out = pltpu.roll(v, (-step) % rows, 0)
    if rows == count:
        return out
    if step == 1:
        other, edge = pltpu.roll(v, count - 1, 0), count - 1
    else:
        other, edge = pltpu.roll(v, rows - (count - 1), 0), 0
    spot = iota(v.shape, 0) & (count - 1)
    return jnp.where(spot == edge, other, out)


def silu_of(pre):
    half = 0.5 * pre
    return half + half * jnp.tanh(half)


def slope_of(pre):
    half = 0.5 * pre
    bend = jnp.tanh(half)
    return (0.5 + 0.5 * bend) * (1.0 + half * (1.0 - bend))


def prep_kernel(vel_ref, cot_ref, out_ref):
    row, col = iota((64, 128), 0), iota((64, 128), 1)
    mask = (row & 7) == (col >> 4)
    spread = one_hot((iota((64, 8), 0) >> 3) == iota((64, 8), 1))
    total = jnp.zeros((64, 128), F32)
    for part, ref in ((0, vel_ref), (1, cot_ref)):
        for chan in range(3):
            wide = mm(spread, ref[chan])
            kept = jnp.where(mask, wide, 0.0).astype(BF)
            place = one_hot(
                iota((128, 128), 1) - (part * 48 + chan) == 3 * (iota((128, 128), 0) & 15)
            )
            total = total + mm(kept, place)
    last = total[48:64]
    spare = iota((16, 128), 1) >= 96
    for g in range(3):
        moved = pltpu.roll(last, 96 - 32 * g, 1)
        rows = jnp.where(spare, moved, total[g * 16:(g + 1) * 16]).astype(BF)
        for copy in range(8):
            out_ref[copy, g * 16:(g + 1) * 16, :] = rows


def build_kernel(
    k1_far,
    k2_far,
    k3_far,
    k4_far,
    l4_far,
    l3_far,
    l2_far,
    head_far,
    weights,
    small,
    k1_ref,
    k2_ref,
    k3_ref,
    k4_ref,
    l4_ref,
    l3_ref,
    l2_ref,
    head_ref,
    sems,
):
    far = (k2_far, k3_far, k4_far, k1_far, l4_far, l3_far, l2_far, head_far)
    near = (k2_ref, k3_ref, k4_ref, k1_ref, l4_ref, l3_ref, l2_ref, head_ref)
    copies = [
        pltpu.make_async_copy(source, target, sems.at[i])
        for i, (source, target) in enumerate(zip(far, near))
    ]
    for copy in copies:
        copy.start()
    band = band_matrix()
    valid, b_row, _, chan = packed((256, 128))
    base = jnp.where(valid, iota((256, 128), 1) - 32 * chan - 3 * b_row, -99)
    rowrep, headmask = head_matrices()
    for copy in copies:
        copy.wait()

    def build(kernel_ref, place, outs, ins):
        planes = 128 // ins
        rep = mm(kernel_ref[...], tile_matrix(outs, 256))
        kout = iota((ins, 256), 1) >> log2(outs)
        for ab in range(9):
            a, b = ab // 3, ab % 3
            taps = [rep[(ab * 3 + c) * ins:(ab * 3 + c + 1) * ins] for c in range(3)]
            for k in range(planes):
                block = jnp.zeros((ins, 256), F32)
                for c in range(3):
                    if 0 <= k - c + 1 < planes:
                        block = jnp.where(kout == k - c + 1, taps[c], block)
                start = place + a * 384 + b * 128 + k * ins
                weights[start:start + ins, :] = block.astype(BF)

    build(k2_ref, PLACES["t2"][0], 32, 16)
    build(k3_ref, PLACES["t3"][0], 64, 32)
    build(k4_ref, PLACES["t4"][0], 128, 64)
    small[...] = jnp.zeros(small.shape, F32)
    for c in range(3):
        small[c * 32:c * 32 + 27, :] = mm_tn(k1_ref[c], tile_matrix(16, 256))
    rep1 = small[...].astype(BF)
    for a in range(3):
        block = jnp.zeros((256, 256), F32)
        for c in range(3):
            block = jnp.where(band == c, mm(one_hot(base == 9 * a + c), rep1), block)
        weights[a * 256:(a + 1) * 256, :] = block.astype(BF)

    def lift(lift_ref, up, back, coarse):
        fine, chans = lift_ref.shape
        rep = mm(lift_ref[...], tile_matrix(chans, 256))
        kin = iota((fine, 256), 1) >> log2(chans)
        for k in range(2 * coarse):
            start = PLACES[up][0] + k * fine
            weights[start:start + fine, :] = jnp.where(kin == k // 2, rep, 0.0).astype(BF)
        for k in range(coarse):
            start = PLACES[back][0] + k * fine
            weights[start:start + fine, :] = jnp.where(kin == k, rep, 0.0).astype(BF)

    lift(l4_ref, "f4", "b4", 2)
    lift(l3_ref, "f3", "b3", 4)
    lift(l2_ref, "f2", "b2", 8)
    small[0:16, 0:128] = jnp.zeros((16, 128), F32)
    small[0:3, 0:16] = head_ref[...].astype(F32)
    tileh = one_hot(iota((128, 256), 0) == (iota((128, 256), 1) & 15))
    reph = mm(small[0:16, 0:128].astype(BF), tileh).astype(BF)
    weights[4992:5120, :] = jnp.where(headmask, mm(rowrep, reph), 0.0).astype(BF)


def main_kernel(
    where_ref,
    own_ref,
    tiles_ref,
    twins_ref,
    weights_far,
    pred_ref,
    gradv_ref,
    share_ref,
    xt,
    xc,
    v3,
    pre1,
    act1,
    pre2,
    act2,
    pre3,
    act3,
    p32,
    p33,
    p34,
    skip1,
    carry2,
    carry3,
    back2,
    back3,
    d1,
    d2,
    d3,
    d4,
    ret2,
    tmp,
    ups_a,
    ups_b,
    line,
    pack,
    weights,
    sem,
):
    weights_copy = pltpu.make_async_copy(weights_far, weights, sem)
    weights_copy.start()
    own_part = where_ref[0]
    lane = iota((1, 128), 1)
    band = band_matrix()
    valid, b_row, _, chan_row = packed((256, 16))
    pick = one_hot(valid & (iota((256, 16), 1) == 3 * b_row + chan_row))
    rowrep, headmask = head_matrices()

    pool1, pool2, pool3 = pool_matrix(16), pool_matrix(32), pool_matrix(64)

    def rows(start, count, unit):
        return pl.ds(pl.multiple_of(start, unit), count)

    v3[0:64, :] = jnp.zeros((64, 256), BF)
    v3[73 * 64:74 * 64, :] = jnp.zeros((64, 256), BF)

    def arrange(source, number, slot):
        lead = slot * 520 + 8
        for n in range(8):
            tile = source(n).astype(F32)
            last = jnp.zeros((16, 128), F32)
            for g in range(3):
                moved = pltpu.roll(tile[g * 16:(g + 1) * 16], 32 * (g + 1), 1)
                last = jnp.where((lane >= 32 * g) & (lane < 32 * g + 32), moved, last)
            for i in range(8):
                piece = tile[i * 8:i * 8 + 8] if i < 6 else last[(i - 6) * 8:(i - 5) * 8]
                xt[lead + i * 64 + n * 8:lead + i * 64 + n * 8 + 8, :] = piece
        for i in range(8):
            place = lead + i * 64
            row = xt[place:place + 64, :]
            xc[rows((number * 8 + i) * 64, 64, 64), :] = row.astype(BF)
            before = jnp.where(spot_y == 0, row[63:64], xt[place - 1:place + 63, :])
            after = jnp.where(spot_y == 63, row[0:1], xt[place + 1:place + 65, :])
            moved = pltpu.roll(row, 48, 1)
            low = jnp.where(lane < 48, before, jnp.where(lane < 96, moved, 0.0))
            high = jnp.where(lane < 48, after, 0.0)
            spot = rows((number * 8 + i + 1) * 64, 64, 64)
            v3[spot, 0:128] = low.astype(BF)
            v3[spot, 128:256] = high.astype(BF)

    def arrange_pairs(turn, _):
        for half in range(2):
            step = turn * 2 + half
            arrange(lambda n: tiles_ref[step, n], where_ref[1 + step], half)
            arrange(lambda n: twins_ref[step, n], where_ref[5 + step], half + 2)
        return 0

    spot_y = iota((64, 128), 0)
    arrange(lambda n: own_ref[n], 4, 0)
    lax.fori_loop(0, 2, arrange_pairs, 0)
    weights_copy.wait()

    def pooled(field, matrix, count, slot=0):
        flat = mm(field, matrix)
        pairs = field.shape[0] // (2 * count)
        lead = slot * 256
        for i in range(pairs):
            tmp[lead + i * count:lead + (i + 1) * count, :] = (
                flat[2 * i * count:(2 * i + 1) * count] + flat[(2 * i + 1) * count:(2 * i + 2) * count]
            )
        n = pairs * count // 2
        return tmp[pl.ds(lead, n, stride=2), :] + tmp[pl.ds(lead + 1, n, stride=2), :]

    def enlarged(field, count):
        n = field.shape[0]
        for half, ref in ((0, ups_a), (1, ups_b)):
            piece = field[:, half * 128:(half + 1) * 128]
            ref[pl.ds(0, n, stride=2), :] = piece
            ref[pl.ds(1, n, stride=2), :] = piece
        big = jnp.concatenate([ups_a[0:2 * n, :], ups_b[0:2 * n, :]], axis=1)
        wide = 2 * count
        parts = []
        for i in range(n // count):
            piece = big[i * wide:(i + 1) * wide]
            parts += [piece, piece]
        return jnp.concatenate(parts, axis=0)

    def put3(ref, start, unit, field, count):
        spot = rows(start, field.shape[0], unit)
        kind = ref.dtype
        ref[spot, 0:128] = shift_y(field, count, -1).astype(kind)
        ref[spot, 128:256] = field.astype(kind)
        ref[spot, 256:384] = shift_y(field, count, 1).astype(kind)

    def fine_forward(turn, _):
        for slot in range(3):
            step = turn * 3 + slot
            start = step * 512
            pre = joint([v3[rows(start + a * 64, 512, 64), :] for a in range(3)], weights, "t1")
            pre1[rows(start, 512, 512), :] = pre
            act = silu_of(pre).astype(BF)
            act1[rows(start, 512, 512), :] = act
            half = (pooled(act, pool1, 64, slot) * 0.125).astype(BF).astype(F32)
            put3(p32, step * 128, 32, half, 32)
        return 0

    lax.fori_loop(0, 3, fine_forward, 0)

    def mid_forward(turn, _):
        for slot in range(2):
            step = turn * 2 + slot
            start = (2 + step * 8) * 32
            pre = joint([p32[rows(start + (a - 1) * 32, 256, 32), :] for a in range(3)], weights, "t2")
            pre2[rows(start, 256, 32), :] = pre
            act = silu_of(pre).astype(BF)
            act2[rows(start, 256, 32), :] = act
            half = (pooled(act, pool2, 32, slot) * 0.125).astype(BF).astype(F32)
            put3(p33, (1 + step * 4) * 16, 16, half, 16)
        return 0

    lax.fori_loop(0, 2, mid_forward, 0)

    pre = joint([p33[(1 + a) * 16:(1 + a) * 16 + 224, :] for a in range(3)], weights, "t3")
    pre3[...] = pre
    act = silu_of(pre).astype(BF)
    act3[...] = act
    half = (pooled(act, pool3, 16) * 0.125).astype(BF).astype(F32)
    put3(p34, 8, 8, half, 8)

    pre4 = joint([p34[(1 + a) * 8:(1 + a) * 8 + 40, :].astype(BF) for a in range(3)], weights, "t4")
    act4 = silu_of(pre4)[16:24].astype(BF)

    skip3 = (act3[96:128, :].astype(F32) + enlarged(mm_nt(act4, taken(weights, "f4")), 8)).astype(BF)
    skip2 = (act2[512:640, :].astype(F32) + enlarged(mm_nt(skip3, taken(weights, "f3")), 16)).astype(BF)
    up2 = mm_nt(skip2, taken(weights, "f2"))
    for half in range(2):
        base = act1[2048 + half * 256:2304 + half * 256, :].astype(F32)
        up = enlarged(up2[half * 64:(half + 1) * 64], 32)
        skip1[half * 256:(half + 1) * 256, :] = (base + up).astype(BF)
    gh = mm_tn(xc[2048:2560, :], skip1[...])

    for step in range(5):
        back = mm(xc[(16 + step * 8) * 64:(24 + step * 8) * 64, :], taken(weights, "hp")).astype(BF)
        carry2[(8 + step * 4) * 32:(12 + step * 4) * 32, :] = pooled(back, pool1, 64, step).astype(BF)

    for step in range(5):
        start = (8 + step * 4) * 32
        back = mm(carry2[start:start + 128, :], taken(weights, "b2")).astype(BF)
        back2[start:start + 128, :] = back
        carry3[step * 32:(step + 1) * 32, :] = pooled(back, pool2, 32, step).astype(BF)
    back = mm(carry3[...], taken(weights, "b3")).astype(BF)
    back3[...] = back
    carry4 = pooled(back, pool3, 16)

    gl2 = mm_tn(carry2[512:640, :], skip2)
    gl3 = mm_tn(carry3[64:96, :], skip3)
    gl4 = mm_tn(carry4[16:24].astype(BF), act4)

    delta4 = (mm(carry4.astype(BF), taken(weights, "b4")) * slope_of(pre4)).astype(BF).astype(F32)
    d4[...] = delta4
    own4 = delta4[16:24].astype(BF)

    def returned(total, count):
        return (
            shift_y(total[:, 0:128], count, 1)
            + total[:, 128:256]
            + shift_y(total[:, 256:384], count, -1)
        )

    total = joint_nt([d4[(2 - a) * 8:(2 - a) * 8 + 24, :].astype(BF) for a in range(3)], weights, "t4")
    ret4 = returned(total, 8)

    def spread_up(field, matrix, count):
        high, low = halves(field * 0.125)
        return enlarged(mm_nt(high, matrix) + mm_nt(low, matrix), count)

    slope = back3[32:128, :].astype(F32) + spread_up(ret4, pool3, 8)
    d3[...] = (slope * slope_of(pre3[64:160, :])).astype(BF)
    total = joint_nt([d3[(2 - a) * 16:(2 - a) * 16 + 64, :] for a in range(3)], weights, "t3")
    ret3 = returned(total, 16)

    slope = back2[14 * 32:22 * 32, :].astype(F32) + spread_up(ret3, pool2, 16)
    d2[...] = (slope * slope_of(pre2[14 * 32:22 * 32, :])).astype(BF)
    total = joint_nt([d2[(2 - a) * 32:(2 - a) * 32 + 192, :] for a in range(3)], weights, "t2")
    ret2[...] = returned(total, 32)

    for step in range(3):
        spot = slice((30 + step * 4) * 64, (34 + step * 4) * 64)
        up = spread_up(ret2[step * 64:(step + 1) * 64, :], pool1, 32)
        back = mm(xc[spot, :], taken(weights, "hp")).astype(BF).astype(F32)
        d1[step * 256:(step + 1) * 256, :] = ((back + up) * slope_of(pre1[spot, :])).astype(BF)

    guess = mm_nt(skip1[...], taken(weights, "hp"))
    total = joint_nt([d1[(3 - a) * 64:(3 - a) * 64 + 512, :] for a in range(3)], weights, "t1")
    low, high = total[:, 0:128], total[:, 128:256]
    grad = shift_y(low, 64, 1) + pltpu.roll(low, 80, 1) + shift_y(high, 64, -1)
    line[...] = jnp.where(lane < 48, grad, guess)
    pieces = [line[rows(i * 64 + own_part * 8, 8, 8), :] for i in range(8)]
    own = jnp.concatenate(pieces, axis=0)
    first, rest = halves(own)
    second, third = halves(own - first.astype(F32))
    mask = (iota((64, 128), 0) & 7) == (iota((64, 128), 1) >> 4)
    for part, ref in ((0, gradv_ref), (1, pred_ref)):
        for chan in range(3):
            matrix = one_hot(
                iota((128, 128), 0) - (part * 48 + chan) == 3 * (iota((128, 128), 1) & 15)
            )
            full = mm(first, matrix) + mm(second, matrix) + mm(third, matrix)
            full = jnp.where(mask, full, 0.0).reshape(8, 8, 128)
            ref[chan] = jnp.sum(full, axis=1)

    pack[1728:PACK, :] = jnp.zeros((PACK - 1728, 128), F32)

    def fold_taps(product, outs, ins, a, b):
        planes = 128 // ins
        kout = iota((ins, 256), 1) >> log2(outs)
        sums = [jnp.zeros((ins, 256), F32) for _ in range(3)]
        for k in range(planes):
            block = product[b * 128 + k * ins:b * 128 + (k + 1) * ins]
            for c in range(3):
                if 0 <= k - c + 1 < planes:
                    sums[c] = sums[c] + jnp.where(kout == k - c + 1, block, 0.0)
        joined = jnp.concatenate(sums, axis=0)
        joined = joined[:, 0:128] + joined[:, 128:256]
        width = outs
        while width < 128:
            joined = joined + pltpu.roll(joined, 128 - width, 1)
            width *= 2
        return joined

    fold4, fold2 = fold_matrix(256, 128, 0), fold_matrix(256, 32, 64)
    for a in range(3):
        product = mm_tn(p34[(3 + a) * 8:(4 + a) * 8, :].astype(BF), own4)
        for b in range(3):
            start = (a * 3 + b) * 192
            pack[start:start + 192, :] = fold_taps(product, 128, 64, a, b)
    for a in range(3):
        product = mm_tn(p33[(7 + a) * 16:(9 + a) * 16, :], d3[32:64, :])
        for b in range(3):
            part = fold_taps(product, 64, 32, a, b)
            left = jnp.where(lane < 64, part, 0.0)
            start = 1728 + (a * 3 + b) * 96
            if a * 3 + b < 8:
                pack[start:start + 96, :] = left
            else:
                pack[2496:2560, :] = left[0:64]
                pack[2352:2384, :] += jnp.where(lane >= 64, part[64:96], 0.0)
    for a in range(3):
        product = mm_tn(p32[(15 + a) * 32:(19 + a) * 32, :], d2[64:192, :])
        for b in range(3):
            part = fold_taps(product, 32, 16, a, b)
            start = 1728 + (a * 3 + b) * 48
            pack[start:start + 48, :] += jnp.where((lane >= 64) & (lane < 96), part, 0.0)
    merged = jnp.zeros((256, 128), F32)
    for a in range(3):
        product = mm_tn(v3[(32 + a) * 64:(40 + a) * 64, :], d1[128:640, :])
        for c in range(3):
            part = jnp.where(band == c, product, 0.0)
            part = part[:, 0:128] + part[:, 128:256]
            for width in (64, 32, 16):
                part = part + pltpu.roll(part, width, 1)
            order = a * 3 + c
            if order < 8:
                merged = jnp.where((lane >> 4) == order, part, merged)
    sums = []
    for field in (merged, part):
        high, low = halves(field)
        sums.append(mm_tn(pick, high) + mm_tn(pick, low))
    for order in range(9):
        block = sums[order // 8]
        shift = (96 - order % 8 * 16) % 128
        block = pltpu.roll(block, shift, 1) if shift else block
        start = 1728 + order * 16
        pack[start:start + 16, :] += jnp.where((lane >= 96) & (lane < 112), block, 0.0)

    def fold_lift(product, fine, chans, matrix):
        kin = iota((fine, 256), 1) >> log2(chans)
        total = jnp.zeros((fine, 256), F32)
        for k in range(256 // chans):
            total = total + jnp.where(kin == k, product[k * fine:(k + 1) * fine], 0.0)
        return mm2(total, matrix)

    pack[2160:2192, :] += fold_lift(gl3, 32, 64, fold_matrix(256, 64, 64))
    pack[2192:2208, :] += fold_lift(gl2, 16, 32, fold2)
    high, low = halves(jnp.where(headmask, gh, 0.0))
    heads = mm_tn(rowrep, high) + mm_tn(rowrep, low)
    pack[2208:2224, :] += mm2(heads, fold_matrix(256, 16, 64))
    lift4 = fold_lift(gl4, 64, 128, fold4)
    pack[2224:2288, :] += jnp.where(lane >= 64, pltpu.roll(lift4, 64, 1), 0.0)
    pack[2288:2352, :] += jnp.where(lane >= 64, lift4, 0.0)
    share_ref[...] = pack[rows(where_ref[9] * SHARE, SHARE, SHARE), :].astype(BF)


def unpack_kernel(
    full_ref, g1_ref, g2_ref, g3_ref, g4_ref, l4_ref, l3_ref, l2_ref, head_ref
):
    scale = float(512 * 64 * 16) ** -0.5
    row, col = iota((144, 128), 0), iota((144, 128), 1)
    a_step, spot = row >> 4, row & 15
    b_row, a_row = (spot * 11) >> 5, (a_step * 11) >> 5
    tap = 9 * a_row + 3 * b_row + a_step - 3 * a_row
    chan = jnp.where(spot < 9, spot - 3 * b_row, -1)

    def left(start, count):
        return full_ref[start:start + count, :].astype(F32) * scale

    def right(start, count):
        return pltpu.roll(left(start, count), 64, 1)

    g4_ref[...] = left(0, 1728)
    g3_ref[0:832, :] = left(1728, 832)[:, 0:64]
    g3_ref[832:864, :] = right(2352, 32)[:, 0:64]
    g2_ref[...] = right(1728, 432)[:, 0:32]
    for c in range(3):
        turned = mm_tn(full_ref[1728:1872, :], one_hot((chan == c) & (col == tap))) * scale
        g1_ref[c] = turned[96:112, 0:27]
    l3_ref[...] = right(2160, 32)[:, 0:64]
    l2_ref[...] = right(2192, 16)[:, 0:32]
    head_ref[...] = right(2208, 16)[0:3, 0:16]
    l4_ref[:, 0:64] = right(2224, 64)[:, 0:64]
    l4_ref[:, 64:128] = left(2288, 64)[:, 64:128]


def run_build(weights, interpret=False):
    k1, k2, k3, k4, l4, l3, l2, head = weights
    return pl.pallas_call(
        build_kernel,
        out_shape=jax.ShapeDtypeStruct((WEIGHT_ROWS, 256), BF),
        in_specs=[pl.BlockSpec(memory_space=pltpu.HBM)] * 8,
        scratch_shapes=[
            pltpu.VMEM((128, 256), F32),
            pltpu.VMEM((3, 16, 27), BF),
            pltpu.VMEM((432, 32), BF),
            pltpu.VMEM((864, 64), BF),
            pltpu.VMEM((1728, 128), BF),
            pltpu.VMEM((64, 128), BF),
            pltpu.VMEM((32, 64), BF),
            pltpu.VMEM((16, 32), BF),
            pltpu.VMEM((3, 16), BF),
            pltpu.SemaphoreType.DMA((8,)),
        ],
        compiler_params=pltpu.CompilerParams(vmem_limit_bytes=60 * 1024 * 1024),
        interpret=interpret,
    )(
        k1.transpose(2, 1, 0),
        k2.transpose(0, 2, 1).reshape(432, 32),
        k3.transpose(0, 2, 1).reshape(864, 64),
        k4.transpose(0, 2, 1).reshape(1728, 128),
        l4,
        l3,
        l2,
        head,
    )


def run_main(where, own, tiles, twins, matrix, interpret=False):
    vm = pl.BlockSpec(memory_space=pltpu.VMEM)

    def buf(shape, kind=BF):
        return pltpu.VMEM(shape, kind)

    scratch = [
        buf((4 * 520 + 16, 128), F32),
        buf((72 * 64, 128)),
        buf((74 * 64, 256)),
        buf((72 * 64, 256), F32),
        buf((72 * 64, 256)),
        buf((36 * 32, 256), F32),
        buf((36 * 32, 256)),
        buf((224, 256), F32),
        buf((224, 256)),
        buf((36 * 32, 384)),
        buf((18 * 16, 384)),
        buf((9 * 8, 384), F32),
        buf((512, 256)),
        buf((36 * 32, 128)),
        buf((160, 128)),
        buf((36 * 32, 256)),
        buf((160, 256)),
        buf((768, 256)),
        buf((256, 256)),
        buf((96, 256)),
        buf((40, 256), F32),
        buf((192, 128), F32),
        buf((5 * 256, 128), F32),
        buf((128, 128), F32),
        buf((128, 128), F32),
        buf((512, 128), F32),
        buf((PACK, 128), F32),
        buf((WEIGHT_ROWS, 256)),
        pltpu.SemaphoreType.DMA,
    ]
    return pl.pallas_call(
        main_kernel,
        out_shape=(
            jax.ShapeDtypeStruct((3, 8, 128), F32),
            jax.ShapeDtypeStruct((3, 8, 128), F32),
            jax.ShapeDtypeStruct((SHARE, 128), BF),
        ),
        in_specs=[pl.BlockSpec(memory_space=pltpu.SMEM)] + [vm] * 3 + [pl.BlockSpec(memory_space=pltpu.HBM)],
        out_specs=(vm, vm, vm),
        scratch_shapes=scratch,
        compiler_params=pltpu.CompilerParams(vmem_limit_bytes=52 * 1024 * 1024),
        interpret=interpret,
    )(
        where,
        own,
        tiles,
        twins,
        matrix,
    )


def run_prep(velocity, cotangent, interpret=False):
    return pl.pallas_call(
        prep_kernel,
        out_shape=jax.ShapeDtypeStruct((8, 48, 128), BF),
        interpret=interpret,
    )(velocity, cotangent)


def unpack(full, interpret=False):
    shapes = ((3, 16, 27), (432, 32), (864, 64), (1728, 128), (64, 128), (32, 64), (16, 32), (3, 16))
    g1, g2, g3, g4, l4, l3, l2, head = pl.pallas_call(
        unpack_kernel,
        out_shape=tuple(jax.ShapeDtypeStruct(shape, F32) for shape in shapes),
        interpret=interpret,
    )(full)
    return (
        g1.transpose(2, 1, 0),
        g2.reshape(27, 16, 32).transpose(0, 2, 1),
        g3.reshape(27, 32, 64).transpose(0, 2, 1),
        g4.reshape(27, 64, 128).transpose(0, 2, 1),
        l4,
        l3,
        l2,
        head,
    )


FAR = (4, -1, -4, 1, 3, -2, -3, 2)
GROUP_Y = [[8 * z + y for y in range(8)] for z in range(8)]
GROUP_Z = [[8 * z + y for z in range(8)] for y in range(8)]


def shared(x):
    copies = jnp.broadcast_to(x, (4,) + x.shape)
    groups = [[0, 2, 4, 6], [1, 3, 5, 7]]
    return lax.all_to_all(copies, "narrow", 0, 0, axis_index_groups=groups, tiled=True)


def exchange(x, groups):
    return lax.all_to_all(x, "wide", 0, 0, axis_index_groups=groups, tiled=True)


def local(velocity, cotangent, *weights):
    part = lax.axis_index("narrow")
    even, odd = ([4 + step for step in FAR[core::2]] for core in range(2))
    order = [jnp.where(part % 2 == 0, a, b) for a, b in zip(even + odd, odd + even)]
    where = jnp.stack([part] + order + [part // 2]).astype(jnp.int32)
    copies = run_prep(velocity, cotangent)
    own = lax.all_to_all(copies, "narrow", 0, 0, tiled=True)
    routes = [((w + FAR[n]) % 64 * 8 + n, w * 8 + n) for w in range(64) for n in range(8)]
    far = lax.ppermute(own, ("wide", "narrow"), routes)
    far, matrix = lax.optimization_barrier((far, run_build(weights)))
    tiles = shared(far)
    twins = lax.ppermute(tiles, "narrow", [(n, n ^ 1) for n in range(8)])
    prediction, grad_velocity, share = run_main(where, own, tiles, twins, matrix)
    pieces = exchange(share.reshape(8, PIECE, 128), GROUP_Y)
    partial = pieces.astype(F32).sum(axis=0).astype(BF)
    pieces = exchange(jnp.broadcast_to(partial, (8, PIECE, 128)), GROUP_Z)
    total = pieces.astype(F32).sum(axis=0).astype(BF)
    whole = exchange(jnp.broadcast_to(total, (8, PIECE, 128)), GROUP_Y).reshape(SHARE, 128)
    return (prediction, grad_velocity) + unpack(shared(whole).reshape(PACK, 128))


def solution(mesh):
    split = P(None, "wide", "narrow")
    return jax.shard_map(
        local,
        mesh=mesh,
        in_specs=(split, split) + (P(),) * 8,
        out_specs=(split, split) + (P(),) * 8,
        check_vma=False,
    )
```

```python
import jax
import jax.numpy as jnp
from jax import lax
from jax.experimental import pallas as pl
from jax.experimental.pallas import tpu as pltpu
from jax.sharding import PartitionSpec as P

BF = jnp.bfloat16
F32 = jnp.float32
NZ = 16
LINES = 9
PIECE = 80
SHARE = 8 * PIECE
PACK = 4 * SHARE
PLACES = {
    "t1": (0, 256),
    "t2": (768, 384),
    "t3": (1920, 384),
    "t4": (3072, 384),
    "f4": (4224, 256),
    "f3": (4480, 256),
    "f2": (4736, 256),
    "hp": (4992, 128),
    "b4": (5120, 128),
    "b3": (5248, 128),
    "b2": (5376, 128),
}
WEIGHT_ROWS = 5504


def mm(a, b):
    return lax.dot_general(a, b, (((1,), (0,)), ((), ())), preferred_element_type=F32)


def mm_nt(a, b):
    return lax.dot_general(a, b, (((1,), (1,)), ((), ())), preferred_element_type=F32)


def mm_tn(a, b):
    return lax.dot_general(a, b, (((0,), (0,)), ((), ())), preferred_element_type=F32)


def halves(x):
    high = x.astype(BF)
    return high, (x - high.astype(F32)).astype(BF)


def taken(weights, name):
    start, count = PLACES[name]
    return weights[start:start + count, :]


def joint(parts, weights, name):
    start, count = PLACES[name]
    return mm(jnp.concatenate(parts, axis=1), weights[start:start + 3 * count, :])


def joint_nt(parts, weights, name):
    start, count = PLACES[name]
    matrix = [weights[start + a * count:start + (a + 1) * count, :] for a in range(3)]
    return mm_nt(jnp.concatenate(parts, axis=1), jnp.concatenate(matrix, axis=1))


def mm2(x, e):
    high, low = halves(x)
    return mm(high, e) + mm(low, e)


def iota(shape, axis):
    return lax.broadcasted_iota(jnp.int32, shape, axis)


def log2(n):
    return int(n).bit_length() - 1


def one_hot(mask):
    return jnp.where(mask, 1.0, 0.0).astype(BF)


def pool_matrix(chans):
    row, col = iota((256, 128), 0), iota((256, 128), 1)
    shift = log2(chans)
    same = (row & (chans - 1)) == (col & (chans - 1))
    return one_hot(same & ((row >> (shift + 1)) == (col >> shift)))


def tile_matrix(chans, lanes):
    return one_hot(iota((chans, lanes), 0) == (iota((chans, lanes), 1) & (chans - 1)))


def fold_matrix(rows, chans, lead):
    row, col = iota((rows, 128), 0), iota((rows, 128), 1)
    return one_hot((row & (chans - 1)) + lead == col)


def packed(shape):
    row = iota(shape, 0)
    b = jnp.where(row < 48, 0, jnp.where(row < 96, 1, 2))
    left = row - jnp.where(row < 48, 0, jnp.where(row < 96, 48, 128))
    kin = (left * 43) >> 7
    valid = (row < 96) | ((row >= 128) & (row < 176))
    return valid, b, kin, left - 3 * kin


def band_matrix():
    valid, _, kin, _ = packed((256, 256))
    return jnp.where(valid, kin - (iota((256, 256), 1) >> 4) + 1, -9)


def head_matrices():
    row = iota((128, 16), 0)
    _, _, _, chan = packed((128, 16))
    second = (row >= 48) & (row < 96)
    rowrep = one_hot(second & (chan == iota((128, 16), 1)))
    row = iota((128, 256), 0)
    _, _, kin, _ = packed((128, 256))
    second = (row >= 48) & (row < 96)
    return rowrep, second & (kin == (iota((128, 256), 1) >> 4))


def shift_y(v, count, step):
    rows = v.shape[0]
    out = pltpu.roll(v, (-step) % rows, 0)
    if rows == count:
        return out
    if step == 1:
        other, edge = pltpu.roll(v, count - 1, 0), count - 1
    else:
        other, edge = pltpu.roll(v, rows - (count - 1), 0), 0
    spot = iota(v.shape, 0) & (count - 1)
    return jnp.where(spot == edge, other, out)


def silu_of(pre):
    half = 0.5 * pre
    return half + half * jnp.tanh(half)


def slope_of(pre):
    half = 0.5 * pre
    bend = jnp.tanh(half)
    return (0.5 + 0.5 * bend) * (1.0 + half * (1.0 - bend))


def prep_kernel(vel_ref, cot_ref, out_ref):
    row, col = iota((64, 128), 0), iota((64, 128), 1)
    mask = (row & 7) == (col >> 4)
    spread = one_hot((iota((64, 8), 0) >> 3) == iota((64, 8), 1))
    total = jnp.zeros((64, 128), F32)
    for part, ref in ((0, vel_ref), (1, cot_ref)):
        for chan in range(3):
            wide = mm(spread, ref[chan])
            kept = jnp.where(mask, wide, 0.0).astype(BF)
            place = one_hot(
                iota((128, 128), 1) - (part * 48 + chan) == 3 * (iota((128, 128), 0) & 15)
            )
            total = total + mm(kept, place)
    last = total[48:64]
    spare = iota((16, 128), 1) >= 96
    for g in range(3):
        moved = pltpu.roll(last, 96 - 32 * g, 1)
        rows = jnp.where(spare, moved, total[g * 16:(g + 1) * 16]).astype(BF)
        for copy in range(8):
            out_ref[copy, g * 16:(g + 1) * 16, :] = rows


def build_kernel(
    k1_far,
    k2_far,
    k3_far,
    k4_far,
    l4_far,
    l3_far,
    l2_far,
    head_far,
    weights,
    small,
    k1_ref,
    k2_ref,
    k3_ref,
    k4_ref,
    l4_ref,
    l3_ref,
    l2_ref,
    head_ref,
    sems,
):
    far = (k2_far, k3_far, k4_far, k1_far, l4_far, l3_far, l2_far, head_far)
    near = (k2_ref, k3_ref, k4_ref, k1_ref, l4_ref, l3_ref, l2_ref, head_ref)
    copies = [
        pltpu.make_async_copy(source, target, sems.at[i])
        for i, (source, target) in enumerate(zip(far, near))
    ]
    for copy in copies:
        copy.start()
    band = band_matrix()
    valid, b_row, _, chan = packed((256, 128))
    base = jnp.where(valid, iota((256, 128), 1) - 32 * chan - 3 * b_row, -99)
    rowrep, headmask = head_matrices()
    for copy in copies:
        copy.wait()

    def build(kernel_ref, place, outs, ins):
        planes = 128 // ins
        rep = mm(kernel_ref[...], tile_matrix(outs, 256))
        kout = iota((ins, 256), 1) >> log2(outs)
        for ab in range(9):
            a, b = ab // 3, ab % 3
            taps = [rep[(ab * 3 + c) * ins:(ab * 3 + c + 1) * ins] for c in range(3)]
            for k in range(planes):
                block = jnp.zeros((ins, 256), F32)
                for c in range(3):
                    if 0 <= k - c + 1 < planes:
                        block = jnp.where(kout == k - c + 1, taps[c], block)
                start = place + a * 384 + b * 128 + k * ins
                weights[start:start + ins, :] = block.astype(BF)

    build(k2_ref, PLACES["t2"][0], 32, 16)
    build(k3_ref, PLACES["t3"][0], 64, 32)
    build(k4_ref, PLACES["t4"][0], 128, 64)
    small[...] = jnp.zeros(small.shape, F32)
    for c in range(3):
        small[c * 32:c * 32 + 27, :] = mm_tn(k1_ref[c], tile_matrix(16, 256))
    rep1 = small[...].astype(BF)
    for a in range(3):
        block = jnp.zeros((256, 256), F32)
        for c in range(3):
            block = jnp.where(band == c, mm(one_hot(base == 9 * a + c), rep1), block)
        weights[a * 256:(a + 1) * 256, :] = block.astype(BF)

    def lift(lift_ref, up, back, coarse):
        fine, chans = lift_ref.shape
        rep = mm(lift_ref[...], tile_matrix(chans, 256))
        kin = iota((fine, 256), 1) >> log2(chans)
        for k in range(2 * coarse):
            start = PLACES[up][0] + k * fine
            weights[start:start + fine, :] = jnp.where(kin == k // 2, rep, 0.0).astype(BF)
        for k in range(coarse):
            start = PLACES[back][0] + k * fine
            weights[start:start + fine, :] = jnp.where(kin == k, rep, 0.0).astype(BF)

    lift(l4_ref, "f4", "b4", 2)
    lift(l3_ref, "f3", "b3", 4)
    lift(l2_ref, "f2", "b2", 8)
    small[0:16, 0:128] = jnp.zeros((16, 128), F32)
    small[0:3, 0:16] = head_ref[...].astype(F32)
    tileh = one_hot(iota((128, 256), 0) == (iota((128, 256), 1) & 15))
    reph = mm(small[0:16, 0:128].astype(BF), tileh).astype(BF)
    weights[4992:5120, :] = jnp.where(headmask, mm(rowrep, reph), 0.0).astype(BF)


def main_kernel(
    where_ref,
    own_ref,
    tiles_ref,
    twins_ref,
    weights_far,
    pred_ref,
    gradv_ref,
    share_ref,
    xt,
    xc,
    v3,
    pre1,
    act1,
    pre2,
    act2,
    pre3,
    act3,
    p32,
    p33,
    p34,
    skip1,
    carry2,
    carry3,
    back2,
    back3,
    d1,
    d2,
    d3,
    d4,
    ret2,
    tmp,
    ups_a,
    ups_b,
    line,
    pack,
    weights,
    sem,
):
    weights_copy = pltpu.make_async_copy(weights_far, weights, sem)
    weights_copy.start()
    own_part = where_ref[0]
    lane = iota((1, 128), 1)
    band = band_matrix()
    valid, b_row, _, chan_row = packed((256, 16))
    pick = one_hot(valid & (iota((256, 16), 1) == 3 * b_row + chan_row))
    rowrep, headmask = head_matrices()

    pool1, pool2, pool3 = pool_matrix(16), pool_matrix(32), pool_matrix(64)

    def rows(start, count, unit):
        return pl.ds(pl.multiple_of(start, unit), count)

    v3[0:64, :] = jnp.zeros((64, 256), BF)
    v3[73 * 64:74 * 64, :] = jnp.zeros((64, 256), BF)

    def arrange(source, number, slot):
        lead = slot * 520 + 8
        for n in range(8):
            tile = source(n).astype(F32)
            last = jnp.zeros((16, 128), F32)
            for g in range(3):
                moved = pltpu.roll(tile[g * 16:(g + 1) * 16], 32 * (g + 1), 1)
                last = jnp.where((lane >= 32 * g) & (lane < 32 * g + 32), moved, last)
            for i in range(8):
                piece = tile[i * 8:i * 8 + 8] if i < 6 else last[(i - 6) * 8:(i - 5) * 8]
                xt[lead + i * 64 + n * 8:lead + i * 64 + n * 8 + 8, :] = piece
        for i in range(8):
            place = lead + i * 64
            row = xt[place:place + 64, :]
            xc[rows((number * 8 + i) * 64, 64, 64), :] = row.astype(BF)
            before = jnp.where(spot_y == 0, row[63:64], xt[place - 1:place + 63, :])
            after = jnp.where(spot_y == 63, row[0:1], xt[place + 1:place + 65, :])
            moved = pltpu.roll(row, 48, 1)
            low = jnp.where(lane < 48, before, jnp.where(lane < 96, moved, 0.0))
            high = jnp.where(lane < 48, after, 0.0)
            spot = rows((number * 8 + i + 1) * 64, 64, 64)
            v3[spot, 0:128] = low.astype(BF)
            v3[spot, 128:256] = high.astype(BF)

    def arrange_pairs(turn, _):
        for half in range(2):
            step = turn * 2 + half
            arrange(lambda n: tiles_ref[step, n], where_ref[1 + step], half)
            arrange(lambda n: twins_ref[step, n], where_ref[5 + step], half + 2)
        return 0

    spot_y = iota((64, 128), 0)
    arrange(lambda n: own_ref[n], 4, 0)
    lax.fori_loop(0, 2, arrange_pairs, 0)
    weights_copy.wait()

    def pooled(field, matrix, count, slot=0):
        flat = mm(field, matrix)
        pairs = field.shape[0] // (2 * count)
        lead = slot * 256
        for i in range(pairs):
            tmp[lead + i * count:lead + (i + 1) * count, :] = (
                flat[2 * i * count:(2 * i + 1) * count] + flat[(2 * i + 1) * count:(2 * i + 2) * count]
            )
        n = pairs * count // 2
        return tmp[pl.ds(lead, n, stride=2), :] + tmp[pl.ds(lead + 1, n, stride=2), :]

    def enlarged(field, count):
        n = field.shape[0]
        for half, ref in ((0, ups_a), (1, ups_b)):
            piece = field[:, half * 128:(half + 1) * 128]
            ref[pl.ds(0, n, stride=2), :] = piece
            ref[pl.ds(1, n, stride=2), :] = piece
        big = jnp.concatenate([ups_a[0:2 * n, :], ups_b[0:2 * n, :]], axis=1)
        wide = 2 * count
        parts = []
        for i in range(n // count):
            piece = big[i * wide:(i + 1) * wide]
            parts += [piece, piece]
        return jnp.concatenate(parts, axis=0)

    def put3(ref, start, unit, field, count):
        spot = rows(start, field.shape[0], unit)
        kind = ref.dtype
        ref[spot, 0:128] = shift_y(field, count, -1).astype(kind)
        ref[spot, 128:256] = field.astype(kind)
        ref[spot, 256:384] = shift_y(field, count, 1).astype(kind)

    def fine_forward(turn, _):
        for slot in range(3):
            step = turn * 3 + slot
            start = step * 512
            pre = joint([v3[rows(start + a * 64, 512, 64), :] for a in range(3)], weights, "t1")
            pre1[rows(start, 512, 512), :] = pre
            act = silu_of(pre).astype(BF)
            act1[rows(start, 512, 512), :] = act
            half = (pooled(act, pool1, 64, slot) * 0.125).astype(BF).astype(F32)
            put3(p32, step * 128, 32, half, 32)
        return 0

    lax.fori_loop(0, 3, fine_forward, 0)

    def mid_forward(turn, _):
        for slot in range(2):
            step = turn * 2 + slot
            start = (2 + step * 8) * 32
            pre = joint([p32[rows(start + (a - 1) * 32, 256, 32), :] for a in range(3)], weights, "t2")
            pre2[rows(start, 256, 32), :] = pre
            act = silu_of(pre).astype(BF)
            act2[rows(start, 256, 32), :] = act
            half = (pooled(act, pool2, 32, slot) * 0.125).astype(BF).astype(F32)
            put3(p33, (1 + step * 4) * 16, 16, half, 16)
        return 0

    lax.fori_loop(0, 2, mid_forward, 0)

    pre = joint([p33[(1 + a) * 16:(1 + a) * 16 + 224, :] for a in range(3)], weights, "t3")
    pre3[...] = pre
    act = silu_of(pre).astype(BF)
    act3[...] = act
    half = (pooled(act, pool3, 16) * 0.125).astype(BF).astype(F32)
    put3(p34, 8, 8, half, 8)

    pre4 = joint([p34[(1 + a) * 8:(1 + a) * 8 + 40, :].astype(BF) for a in range(3)], weights, "t4")
    act4 = silu_of(pre4)[16:24].astype(BF)

    skip3 = (act3[96:128, :].astype(F32) + enlarged(mm_nt(act4, taken(weights, "f4")), 8)).astype(BF)
    skip2 = (act2[512:640, :].astype(F32) + enlarged(mm_nt(skip3, taken(weights, "f3")), 16)).astype(BF)
    up2 = mm_nt(skip2, taken(weights, "f2"))
    for half in range(2):
        base = act1[2048 + half * 256:2304 + half * 256, :].astype(F32)
        up = enlarged(up2[half * 64:(half + 1) * 64], 32)
        skip1[half * 256:(half + 1) * 256, :] = (base + up).astype(BF)
    gh = mm_tn(xc[2048:2560, :], skip1[...])

    for step in range(5):
        back = mm(xc[(16 + step * 8) * 64:(24 + step * 8) * 64, :], taken(weights, "hp")).astype(BF)
        carry2[(8 + step * 4) * 32:(12 + step * 4) * 32, :] = pooled(back, pool1, 64, step).astype(BF)

    for step in range(5):
        start = (8 + step * 4) * 32
        back = mm(carry2[start:start + 128, :], taken(weights, "b2")).astype(BF)
        back2[start:start + 128, :] = back
        carry3[step * 32:(step + 1) * 32, :] = pooled(back, pool2, 32, step).astype(BF)
    back = mm(carry3[...], taken(weights, "b3")).astype(BF)
    back3[...] = back
    carry4 = pooled(back, pool3, 16)

    gl2 = mm_tn(carry2[512:640, :], skip2)
    gl3 = mm_tn(carry3[64:96, :], skip3)
    gl4 = mm_tn(carry4[16:24].astype(BF), act4)

    delta4 = (mm(carry4.astype(BF), taken(weights, "b4")) * slope_of(pre4)).astype(BF).astype(F32)
    d4[...] = delta4
    own4 = delta4[16:24].astype(BF)

    def returned(total, count):
        return (
            shift_y(total[:, 0:128], count, 1)
            + total[:, 128:256]
            + shift_y(total[:, 256:384], count, -1)
        )

    total = joint_nt([d4[(2 - a) * 8:(2 - a) * 8 + 24, :].astype(BF) for a in range(3)], weights, "t4")
    ret4 = returned(total, 8)

    def spread_up(field, matrix, count):
        high, low = halves(field * 0.125)
        return enlarged(mm_nt(high, matrix) + mm_nt(low, matrix), count)

    slope = back3[32:128, :].astype(F32) + spread_up(ret4, pool3, 8)
    d3[...] = (slope * slope_of(pre3[64:160, :])).astype(BF)
    total = joint_nt([d3[(2 - a) * 16:(2 - a) * 16 + 64, :] for a in range(3)], weights, "t3")
    ret3 = returned(total, 16)

    slope = back2[14 * 32:22 * 32, :].astype(F32) + spread_up(ret3, pool2, 16)
    d2[...] = (slope * slope_of(pre2[14 * 32:22 * 32, :])).astype(BF)
    total = joint_nt([d2[(2 - a) * 32:(2 - a) * 32 + 192, :] for a in range(3)], weights, "t2")
    ret2[...] = returned(total, 32)

    for step in range(3):
        spot = slice((30 + step * 4) * 64, (34 + step * 4) * 64)
        up = spread_up(ret2[step * 64:(step + 1) * 64, :], pool1, 32)
        back = mm(xc[spot, :], taken(weights, "hp")).astype(BF).astype(F32)
        d1[step * 256:(step + 1) * 256, :] = ((back + up) * slope_of(pre1[spot, :])).astype(BF)

    guess = mm_nt(skip1[...], taken(weights, "hp"))
    total = joint_nt([d1[(3 - a) * 64:(3 - a) * 64 + 512, :] for a in range(3)], weights, "t1")
    low, high = total[:, 0:128], total[:, 128:256]
    grad = shift_y(low, 64, 1) + pltpu.roll(low, 80, 1) + shift_y(high, 64, -1)
    line[...] = jnp.where(lane < 48, grad, guess)
    pieces = [line[rows(i * 64 + own_part * 8, 8, 8), :] for i in range(8)]
    own = jnp.concatenate(pieces, axis=0)
    first, rest = halves(own)
    second, third = halves(own - first.astype(F32))
    mask = (iota((64, 128), 0) & 7) == (iota((64, 128), 1) >> 4)
    for part, ref in ((0, gradv_ref), (1, pred_ref)):
        for chan in range(3):
            matrix = one_hot(
                iota((128, 128), 0) - (part * 48 + chan) == 3 * (iota((128, 128), 1) & 15)
            )
            full = mm(first, matrix) + mm(second, matrix) + mm(third, matrix)
            full = jnp.where(mask, full, 0.0).reshape(8, 8, 128)
            ref[chan] = jnp.sum(full, axis=1)

    pack[1728:PACK, :] = jnp.zeros((PACK - 1728, 128), F32)

    def fold_taps(product, outs, ins, a, b):
        planes = 128 // ins
        kout = iota((ins, 256), 1) >> log2(outs)
        sums = [jnp.zeros((ins, 256), F32) for _ in range(3)]
        for k in range(planes):
            block = product[b * 128 + k * ins:b * 128 + (k + 1) * ins]
            for c in range(3):
                if 0 <= k - c + 1 < planes:
                    sums[c] = sums[c] + jnp.where(kout == k - c + 1, block, 0.0)
        joined = jnp.concatenate(sums, axis=0)
        joined = joined[:, 0:128] + joined[:, 128:256]
        width = outs
        while width < 128:
            joined = joined + pltpu.roll(joined, 128 - width, 1)
            width *= 2
        return joined

    fold4, fold2 = fold_matrix(256, 128, 0), fold_matrix(256, 32, 64)
    for a in range(3):
        product = mm_tn(p34[(3 + a) * 8:(4 + a) * 8, :].astype(BF), own4)
        for b in range(3):
            start = (a * 3 + b) * 192
            pack[start:start + 192, :] = fold_taps(product, 128, 64, a, b)
    for a in range(3):
        product = mm_tn(p33[(7 + a) * 16:(9 + a) * 16, :], d3[32:64, :])
        for b in range(3):
            part = fold_taps(product, 64, 32, a, b)
            left = jnp.where(lane < 64, part, 0.0)
            start = 1728 + (a * 3 + b) * 96
            if a * 3 + b < 8:
                pack[start:start + 96, :] = left
            else:
                pack[2496:2560, :] = left[0:64]
                pack[2352:2384, :] += jnp.where(lane >= 64, part[64:96], 0.0)
    for a in range(3):
        product = mm_tn(p32[(15 + a) * 32:(19 + a) * 32, :], d2[64:192, :])
        for b in range(3):
            part = fold_taps(product, 32, 16, a, b)
            start = 1728 + (a * 3 + b) * 48
            pack[start:start + 48, :] += jnp.where((lane >= 64) & (lane < 96), part, 0.0)
    merged = jnp.zeros((256, 128), F32)
    for a in range(3):
        product = mm_tn(v3[(32 + a) * 64:(40 + a) * 64, :], d1[128:640, :])
        for c in range(3):
            part = jnp.where(band == c, product, 0.0)
            part = part[:, 0:128] + part[:, 128:256]
            for width in (64, 32, 16):
                part = part + pltpu.roll(part, width, 1)
            order = a * 3 + c
            if order < 8:
                merged = jnp.where((lane >> 4) == order, part, merged)
    sums = []
    for field in (merged, part):
        high, low = halves(field)
        sums.append(mm_tn(pick, high) + mm_tn(pick, low))
    for order in range(9):
        block = sums[order // 8]
        shift = (96 - order % 8 * 16) % 128
        block = pltpu.roll(block, shift, 1) if shift else block
        start = 1728 + order * 16
        pack[start:start + 16, :] += jnp.where((lane >= 96) & (lane < 112), block, 0.0)

    def fold_lift(product, fine, chans, matrix):
        kin = iota((fine, 256), 1) >> log2(chans)
        total = jnp.zeros((fine, 256), F32)
        for k in range(256 // chans):
            total = total + jnp.where(kin == k, product[k * fine:(k + 1) * fine], 0.0)
        return mm2(total, matrix)

    pack[2160:2192, :] += fold_lift(gl3, 32, 64, fold_matrix(256, 64, 64))
    pack[2192:2208, :] += fold_lift(gl2, 16, 32, fold2)
    high, low = halves(jnp.where(headmask, gh, 0.0))
    heads = mm_tn(rowrep, high) + mm_tn(rowrep, low)
    pack[2208:2224, :] += mm2(heads, fold_matrix(256, 16, 64))
    lift4 = fold_lift(gl4, 64, 128, fold4)
    pack[2224:2288, :] += jnp.where(lane >= 64, pltpu.roll(lift4, 64, 1), 0.0)
    pack[2288:2352, :] += jnp.where(lane >= 64, lift4, 0.0)
    share_ref[...] = pack[rows(where_ref[9] * SHARE, SHARE, SHARE), :].astype(BF)


def unpack_kernel(
    full_ref, g1_ref, g2_ref, g3_ref, g4_ref, l4_ref, l3_ref, l2_ref, head_ref
):
    scale = float(512 * 64 * 16) ** -0.5
    row, col = iota((144, 128), 0), iota((144, 128), 1)
    a_step, spot = row >> 4, row & 15
    b_row, a_row = (spot * 11) >> 5, (a_step * 11) >> 5
    tap = 9 * a_row + 3 * b_row + a_step - 3 * a_row
    chan = jnp.where(spot < 9, spot - 3 * b_row, -1)

    def left(start, count):
        return full_ref[start:start + count, :].astype(F32) * scale

    def right(start, count):
        return pltpu.roll(left(start, count), 64, 1)

    g4_ref[...] = left(0, 1728)
    g3_ref[0:832, :] = left(1728, 832)[:, 0:64]
    g3_ref[832:864, :] = right(2352, 32)[:, 0:64]
    g2_ref[...] = right(1728, 432)[:, 0:32]
    for c in range(3):
        turned = mm_tn(full_ref[1728:1872, :], one_hot((chan == c) & (col == tap))) * scale
        g1_ref[c] = turned[96:112, 0:27]
    l3_ref[...] = right(2160, 32)[:, 0:64]
    l2_ref[...] = right(2192, 16)[:, 0:32]
    head_ref[...] = right(2208, 16)[0:3, 0:16]
    l4_ref[:, 0:64] = right(2224, 64)[:, 0:64]
    l4_ref[:, 64:128] = left(2288, 64)[:, 64:128]


def run_build(weights, interpret=False):
    k1, k2, k3, k4, l4, l3, l2, head = weights
    return pl.pallas_call(
        build_kernel,
        out_shape=jax.ShapeDtypeStruct((WEIGHT_ROWS, 256), BF),
        in_specs=[pl.BlockSpec(memory_space=pltpu.HBM)] * 8,
        scratch_shapes=[
            pltpu.VMEM((128, 256), F32),
            pltpu.VMEM((3, 16, 27), BF),
            pltpu.VMEM((432, 32), BF),
            pltpu.VMEM((864, 64), BF),
            pltpu.VMEM((1728, 128), BF),
            pltpu.VMEM((64, 128), BF),
            pltpu.VMEM((32, 64), BF),
            pltpu.VMEM((16, 32), BF),
            pltpu.VMEM((3, 16), BF),
            pltpu.SemaphoreType.DMA((8,)),
        ],
        compiler_params=pltpu.CompilerParams(vmem_limit_bytes=60 * 1024 * 1024),
        interpret=interpret,
    )(
        k1.transpose(2, 1, 0),
        k2.transpose(0, 2, 1).reshape(432, 32),
        k3.transpose(0, 2, 1).reshape(864, 64),
        k4.transpose(0, 2, 1).reshape(1728, 128),
        l4,
        l3,
        l2,
        head,
    )


def run_main(where, own, tiles, twins, matrix, interpret=False):
    vm = pl.BlockSpec(memory_space=pltpu.VMEM)

    def buf(shape, kind=BF):
        return pltpu.VMEM(shape, kind)

    scratch = [
        buf((4 * 520 + 16, 128), F32),
        buf((72 * 64, 128)),
        buf((74 * 64, 256)),
        buf((72 * 64, 256), F32),
        buf((72 * 64, 256)),
        buf((36 * 32, 256), F32),
        buf((36 * 32, 256)),
        buf((224, 256), F32),
        buf((224, 256)),
        buf((36 * 32, 384)),
        buf((18 * 16, 384)),
        buf((9 * 8, 384), F32),
        buf((512, 256)),
        buf((36 * 32, 128)),
        buf((160, 128)),
        buf((36 * 32, 256)),
        buf((160, 256)),
        buf((768, 256)),
        buf((256, 256)),
        buf((96, 256)),
        buf((40, 256), F32),
        buf((192, 128), F32),
        buf((5 * 256, 128), F32),
        buf((128, 128), F32),
        buf((128, 128), F32),
        buf((512, 128), F32),
        buf((PACK, 128), F32),
        buf((WEIGHT_ROWS, 256)),
        pltpu.SemaphoreType.DMA,
    ]
    return pl.pallas_call(
        main_kernel,
        out_shape=(
            jax.ShapeDtypeStruct((3, 8, 128), F32),
            jax.ShapeDtypeStruct((3, 8, 128), F32),
            jax.ShapeDtypeStruct((SHARE, 128), BF),
        ),
        in_specs=[pl.BlockSpec(memory_space=pltpu.SMEM)] + [vm] * 3 + [pl.BlockSpec(memory_space=pltpu.HBM)],
        out_specs=(vm, vm, vm),
        scratch_shapes=scratch,
        compiler_params=pltpu.CompilerParams(vmem_limit_bytes=52 * 1024 * 1024),
        interpret=interpret,
    )(
        where,
        own,
        tiles,
        twins,
        matrix,
    )


def run_prep(velocity, cotangent, interpret=False):
    return pl.pallas_call(
        prep_kernel,
        out_shape=jax.ShapeDtypeStruct((8, 48, 128), BF),
        interpret=interpret,
    )(velocity, cotangent)


def unpack(full, interpret=False):
    shapes = ((3, 16, 27), (432, 32), (864, 64), (1728, 128), (64, 128), (32, 64), (16, 32), (3, 16))
    g1, g2, g3, g4, l4, l3, l2, head = pl.pallas_call(
        unpack_kernel,
        out_shape=tuple(jax.ShapeDtypeStruct(shape, F32) for shape in shapes),
        interpret=interpret,
    )(full)
    return (
        g1.transpose(2, 1, 0),
        g2.reshape(27, 16, 32).transpose(0, 2, 1),
        g3.reshape(27, 32, 64).transpose(0, 2, 1),
        g4.reshape(27, 64, 128).transpose(0, 2, 1),
        l4,
        l3,
        l2,
        head,
    )


FAR = (-1, 4, 1, -4, -2, 3, 2, -3)
GROUP_Y = [[8 * z + y for y in range(8)] for z in range(8)]
GROUP_Z = [[8 * z + y for z in range(8)] for y in range(8)]


def shared(x):
    copies = jnp.broadcast_to(x, (4,) + x.shape)
    groups = [[0, 2, 4, 6], [1, 3, 5, 7]]
    return lax.all_to_all(copies, "narrow", 0, 0, axis_index_groups=groups, tiled=True)


def exchange(x, groups):
    return lax.all_to_all(x, "wide", 0, 0, axis_index_groups=groups, tiled=True)


def local(velocity, cotangent, *weights):
    part = lax.axis_index("narrow")
    even, odd = ([4 + step for step in FAR[core::2]] for core in range(2))
    order = [jnp.where(part % 2 == 0, a, b) for a, b in zip(even + odd, odd + even)]
    where = jnp.stack([part] + order + [part // 2]).astype(jnp.int32)
    copies = run_prep(velocity, cotangent)
    own = lax.all_to_all(copies, "narrow", 0, 0, tiled=True)
    routes = [((w + FAR[n]) % 64 * 8 + n, w * 8 + n) for w in range(64) for n in range(8)]
    far = lax.ppermute(own, ("wide", "narrow"), routes)
    far, matrix = lax.optimization_barrier((far, run_build(weights)))
    tiles = shared(far)
    twins = lax.ppermute(tiles, "narrow", [(n, n ^ 1) for n in range(8)])
    prediction, grad_velocity, share = run_main(where, own, tiles, twins, matrix)
    pieces = exchange(share.reshape(8, PIECE, 128), GROUP_Y)
    partial = pieces.astype(F32).sum(axis=0).astype(BF)
    pieces = exchange(jnp.broadcast_to(partial, (8, PIECE, 128)), GROUP_Z)
    total = pieces.astype(F32).sum(axis=0).astype(BF)
    whole = exchange(jnp.broadcast_to(total, (8, PIECE, 128)), GROUP_Y).reshape(SHARE, 128)
    return (prediction, grad_velocity) + unpack(shared(whole).reshape(PACK, 128))


def solution(mesh):
    split = P(None, "wide", "narrow")
    return jax.shard_map(
        local,
        mesh=mesh,
        in_specs=(split, split) + (P(),) * 8,
        out_specs=(split, split) + (P(),) * 8,
        check_vma=False,
    )
```
